256 devices in a mesh: gx: 32 (over x, y, core), gz: 8 (over z).
Axes of the slice: x: 4, y: 4, z: 8, core: 2. Of those that a mesh axis runs over, the one named last changes fastest.
Arguments:
- potential: float32 [1024, 512, 128], P('gz', 'gx'), may hold values from -3 to 3
- negative_charges: float32 [1024, 512, 128], P('gz', 'gx'), may hold values from 0.1 to 10
- positive_charges: float32 [1024, 512, 128], P('gz', 'gx'), may hold values from 0.1 to 10
- vacancies: float32 [1024, 512, 128], P('gz', 'gx'), may hold values from 0.2 to 5
- permittivity: float32 [1024, 512, 128], P('gz', 'gx'), may hold values from 2 to 30
- doping: float32 [1024, 512, 128], P('gz', 'gx'), may hold values from -6 to 6
- optical_creation: float32 [1024, 512, 128], P('gz', 'gx'), may hold values from 0.1 to 4
- layer: int32 [1024], replicated, may hold values from 0 to 2, as said below
- height: int32 [512, 128], P('gx'), may hold values from 0 to 15
Outputs:
- potential_out: float32 [1024, 512, 128], P('gz', 'gx')
- electrons_out: float32 [1024, 512, 128], P('gz', 'gx')
- holes_out: float32 [1024, 512, 128], P('gz', 'gx')
- vacancies_out: float32 [1024, 512, 128], P('gz', 'gx')
The draws below stay inside these ranges and needn't reach their ends.
Inputs may be any that keep to these rules, and one draw needn't show every extreme that they name: layer never falls along depth: 0 on the first levels, then 1 on a band of a few levels, then 2; all three values occur, and the first 1 lies at depth index under 3 * 128.
All inputs are finite; a program needn't handle non-finite values.
Results may differ from the reference program's by a relative error of at most 0.0003.
Values sent between devices are 32-bit elements; how exact they have to be, the bound alone decides.
A program may use at most 128 MiB of HBM per device.

```python
import math
import jax
import jax.numpy as jnp

NY = 128
HMAX = 16
ITERS = 4
NX = 512
NZ = 1024


def draw_layer(key, part):
    key = jax.random.fold_in(key, 7)
    first_key, second_key = jax.random.split(key)
    boundary = jax.random.randint(first_key, (), NZ // 8, 3 * NZ // 8)
    interface_plane = jax.random.randint(second_key, (), 2, 9)
    depth = jnp.arange(NZ, dtype=jnp.int32)
    return jnp.where(depth < boundary, 0, jnp.where(depth < boundary + interface_plane, 1, 2)).astype(jnp.int32)


def with_ends(result, rng, least, high):
    longest = result.shape.index(max(result.shape))
    spots = []
    for shift in (0, 1):
        where = [jax.random.randint(jax.random.fold_in(rng, axis), (), 0, length) for axis, length in enumerate(result.shape)]
        where[longest] = (where[longest] + shift) % result.shape[longest]
        spots.append(tuple(where))
    return result.at[spots[0]].set(least).at[spots[1]].set(high)


def steps_of(rng, dims, shards, smallest, largest):
    loudness, own = 1.0, jax.random.fold_in(rng, 6)
    for dim, parts in shards:
        draws = jnp.exp(jax.random.uniform(jax.random.fold_in(own, dim), (parts,), jnp.float32, smallest / len(shards), largest / len(shards)))
        loudness = loudness * jnp.repeat(draws, dims[dim] // parts).reshape([-1 if axis == dim else 1 for axis in range(len(dims))])
    return loudness


def bell_draw(stream_key, extent, scale, reach, cuts=(), kind=jnp.bfloat16):
    gain = steps_of(stream_key, extent, cuts, -0.22, 0.18) if cuts else 1.0
    entries = jax.random.normal(stream_key, extent, jnp.float32) * scale * gain
    return jnp.minimum(jnp.maximum(entries, -reach), reach).astype(kind)


def setup_inputs(seed: int = 0) -> dict:
    keys = jax.random.split(jax.random.key(seed), 10)
    potential = bell_draw(keys[0], (NZ, NX, NY), 0.5, 3.0, ((0, 8), (1, 32)), jnp.float32)
    negative_charges = jnp.clip(jnp.exp(math.log(10.0) - 4.6051702 * jax.random.uniform(keys[1], (NZ, NX, NY), jnp.float32) ** steps_of(keys[1], (NZ, NX, NY), ((0, 8), (1, 32)), -0.2, 0.2)), 0.1, 10.0)
    positive_charges = jnp.clip(jnp.exp(math.log(10.0) - 4.6051702 * jax.random.uniform(keys[2], (NZ, NX, NY), jnp.float32) ** steps_of(keys[2], (NZ, NX, NY), ((0, 8), (1, 32)), -0.2, 0.2)), 0.1, 10.0)
    vacancies = jnp.clip(jnp.exp(math.log(5.0) - 3.218876 * jax.random.uniform(keys[3], (NZ, NX, NY), jnp.float32) ** steps_of(keys[3], (NZ, NX, NY), ((0, 8), (1, 32)), -0.2, 0.2)), 0.2, 5.0)
    permittivity = jnp.clip(jnp.exp(math.log(30.0) - 2.7080502 * jax.random.uniform(keys[4], (NZ, NX, NY), jnp.float32) ** steps_of(keys[4], (NZ, NX, NY), ((0, 8), (1, 32)), -0.2, 0.2)), 2.0, 30.0)
    doping = bell_draw(keys[5], (NZ, NX, NY), 1.0, 6.0, ((0, 8), (1, 32)), jnp.float32)
    optical_creation = jnp.clip(jnp.exp(math.log(4.0) - 3.6888794 * jax.random.uniform(keys[6], (NZ, NX, NY), jnp.float32) ** steps_of(keys[6], (NZ, NX, NY), ((0, 8), (1, 32)), -0.2, 0.2)), 0.1, 4.0)
    layer = draw_layer(jax.random.fold_in(keys[9], 71), 0)
    height = with_ends(jax.random.randint(keys[8], (NX, NY), 0, HMAX), jax.random.fold_in(keys[8], 1), 0, HMAX - 1).astype(jnp.int32)
    return dict(potential=potential, negative_charges=negative_charges, positive_charges=positive_charges, vacancies=vacancies, permittivity=permittivity, doping=doping, optical_creation=optical_creation, layer=layer, height=height)


POISSON_SCALE = 2.0
TIME_STEP = 0.05
DIFF_ELEC = 0.8
DIFF_HOLE = 0.6
DIFF_ION = 0.4


def bernoulli(value):
    small = jnp.abs(value) < 1e-3
    safe = jnp.where(small, jnp.ones_like(value), jnp.expm1(value))
    return jnp.where(small, 1.0 - 0.5 * value + value * value / 12.0, value / safe)


def neighbours(extended):
    centre = extended[1:-1, 1:-1]
    return [extended[:-2, 1:-1], extended[2:, 1:-1], extended[1:-1, :-2], extended[1:-1, 2:],
            jnp.roll(centre, 1, axis=2), jnp.roll(centre, -1, axis=2)]


def sweep(voltage_bordered, eps_ext, charge, outside):
    eps_centre = eps_ext[1:-1, 1:-1]
    numer = POISSON_SCALE * charge
    denom = outside
    for eps_next, psi_next in zip(neighbours(eps_ext), neighbours(voltage_bordered)):
        coef = 0.5 * (eps_centre + eps_next)
        numer = numer + coef * psi_next
        denom = denom + coef
    return numer / denom * (1.0 - outside)


def charged_populations(voltage_bordered, negative_bordered, positive_bordered, optical_creation, recombination_time):
    psi_c = voltage_bordered[1:-1, 1:-1]
    negative_middle = negative_bordered[1:-1, 1:-1]
    positive_middle = positive_bordered[1:-1, 1:-1]
    out_elec = jnp.zeros_like(psi_c)
    out_hole = jnp.zeros_like(psi_c)
    floor_limits = []
    voltage_iterates = []
    for psi_n, elec_n, hole_n in zip(neighbours(voltage_bordered), neighbours(negative_bordered), neighbours(positive_bordered)):
        delta = psi_n - psi_c
        lower = bernoulli(delta)
        upper = lower + delta
        out_elec = out_elec + (upper * negative_middle - lower * elec_n)
        out_hole = out_hole + (lower * positive_middle - upper * hole_n)
        floor_limits.append(lower)
        voltage_iterates.append(delta)
    annihilation_loss = (negative_middle * positive_middle - 1.0) / (recombination_time * (negative_middle + positive_middle + 2.0))
    negative_population = negative_middle - TIME_STEP * DIFF_ELEC * out_elec + TIME_STEP * (optical_creation - annihilation_loss)
    positive_population = positive_middle - TIME_STEP * DIFF_HOLE * out_hole + TIME_STEP * (optical_creation - annihilation_loss)
    return negative_population, positive_population, floor_limits, voltage_iterates


def ion_update(ion_ext, pero_ext, floor_limits, voltage_iterates):
    ion_c = ion_ext[1:-1, 1:-1]
    pero_c = pero_ext[1:-1, 1:-1]
    out_ion = jnp.zeros_like(ion_c)
    for lower, delta, ion_n, pero_n in zip(floor_limits, voltage_iterates, neighbours(ion_ext), neighbours(pero_ext)):
        upper = lower + delta
        out_ion = out_ion + (lower * ion_c - upper * ion_n) * (pero_c * pero_n)
    return ion_c - TIME_STEP * DIFF_ION * out_ion


def bordered_mesh(field):
    return jnp.pad(field, ((1, 1), (1, 1), (0, 0)))


def reference(potential, negative_charges, positive_charges, vacancies, permittivity, doping, optical_creation, layer, height):
    depth = jnp.arange(NZ, dtype=jnp.int32)
    level = depth[:, None, None] + height[None]
    substance_label = layer[jnp.minimum(level, NZ - 1).astype(jnp.int32)]
    perovskite = (substance_label == 0).astype(jnp.float32)
    recombination_time = jnp.where(substance_label == 0, 1.0, jnp.where(substance_label == 1, 0.1, 5.0)).astype(jnp.float32)
    ions = vacancies * perovskite
    charge = positive_charges - negative_charges + ions + doping
    eps_ext = bordered_mesh(permittivity)
    psi = potential
    for sweep_index in range(ITERS):
        psi = sweep(bordered_mesh(psi), eps_ext, charge, 0.0)
    voltage_bordered = bordered_mesh(psi)
    negative_population, positive_population, floor_limits, voltage_iterates = charged_populations(voltage_bordered, bordered_mesh(negative_charges), bordered_mesh(positive_charges), optical_creation, recombination_time)
    ion = ion_update(bordered_mesh(ions), bordered_mesh(perovskite), floor_limits, voltage_iterates)
    return psi, negative_population, positive_population, ion
```

```python
import functools

import jax
import jax.numpy as jnp
from jax import lax
from jax.experimental import pallas as pl
from jax.experimental.pallas import tpu as pltpu
from jax.sharding import PartitionSpec as P

MESH = pl.DeviceIdType.MESH
F32 = jnp.float32

NXL = 16
NZL = 128
NY = 128
XO = 3
ZO = 16
PLANES = NXL + 2 * XO
ROWS = NZL + 2 * ZO
LO = ZO - 8
HI = ZO + NZL + 8
SPAN = HI - LO
TINY = 1e-10

XROWS = (ZO, ZO + NZL)
EROWS = (LO, HI)


def x_message(width, first, rows):
    low = XO - first - width
    return (
        ((XO + NXL - first - width, low, width), rows),
        ((XO + first, XO + NXL + first, width), rows),
    )


def row_parts(depth):
    return ((ZO + NZL - depth, ZO - depth, depth), (ZO, ZO + NZL, depth))


def messages():
    table = {}
    for name, buffer, width, first, rows in (
        ("psi", "psi0", 2, 0, XROWS),
        ("eps", "eps", 3, 0, XROWS),
        ("q", "q", 2, 0, XROWS),
        ("n", "n", 1, 0, XROWS),
        ("p", "p", 1, 0, XROWS),
        ("i", "i", 1, 0, XROWS),
        ("psi1", "psi1", 2, 1, EROWS),
        ("psi2", "psi2", 1, 2, EROWS),
    ):
        right, left = x_message(width, first, rows)
        for dx, ((src, dst, count), (lo, hi)) in ((1, right), (-1, left)):
            table.setdefault("x" + name, []).append((buffer, (dx, 0), src, dst, count, lo, lo, hi - lo))
    for name, buffer, depth in (
        ("psi", "psi0", 5),
        ("eps", "eps", 5),
        ("q", "q", 4),
        ("n", "n", 1),
        ("p", "p", 1),
        ("i", "i", 1),
    ):
        for dz, (src, dst, count) in zip((1, -1), row_parts(depth)):
            table.setdefault("z" + name, []).append((buffer, (0, dz), XO, XO, NXL, src, dst, count))
    for name, buffer, width, depth in (("psi", "psi0", 2, 5), ("eps", "eps", 3, 5), ("q", "q", 2, 4)):
        right, left = x_message(width, 0, XROWS)
        for dx, ((xsrc, xdst, xcount), _) in ((1, right), (-1, left)):
            for dz, (src, dst, count) in zip((1, -1), row_parts(depth)):
                table.setdefault("d" + name, []).append((buffer, (dx, dz), xsrc, xdst, xcount, src, dst, count))
    return table


MESSAGES = messages()
INDEX = {}
for _name, _list in MESSAGES.items():
    INDEX[_name] = list(range(sum(map(len, INDEX.values())), sum(map(len, INDEX.values())) + len(_list)))
COUNT = sum(map(len, INDEX.values()))


def blocked(body, first, count, unroll):
    steps = count // unroll
    if steps > 1:

        def step(k, carry):
            for u in range(unroll):
                body(first + k * unroll + u)
            return carry

        lax.fori_loop(0, steps, step, 0)
    else:
        steps = 0
    for u in range(steps * unroll, count):
        body(first + u)


def both_sides(body, first, count, shift):
    def step(side, carry):
        for u in range(count):
            body(first + side * shift + u)
        return carry

    lax.fori_loop(0, 2, step, 0)


def layer_counts(layer_ref):
    kinds = layer_ref[...]

    def total(mask):
        ones = jnp.where(mask, 1.0, 0.0).astype(F32)
        return jnp.sum(jnp.sum(ones, axis=0, keepdims=True), axis=1, keepdims=True)

    return total(kinds == 0), total(kinds <= 1)


def poisson_kernel(
    psi_h, eps_h, n_h, p_h, vac_h, dop_h, layer_ref, height_ref,
    psi4, n_b, p_b, i_b,
    psi0, psi1, psi2, psi3, eps, q, rden, cx, cy, cz, load_sem, send_sem, recv_sem,
):
    gx, gz = lax.axis_index("gx"), lax.axis_index("gz")
    gxs, gzs = lax.axis_size("gx"), lax.axis_size("gz")
    buffers = {"psi0": psi0, "psi1": psi1, "psi2": psi2, "eps": eps, "q": q, "n": n_b, "p": p_b, "i": i_b}

    barrier = pltpu.get_barrier_semaphore()
    for dx in (-1, 0, 1):
        for dz in (-1, 0, 1):
            if dx or dz:
                there = (lax.rem(gx + dx + gxs, gxs), lax.rem(gz + dz + gzs, gzs))
                pl.semaphore_signal(barrier, inc=1, device_id=there, device_id_type=MESH)

    inner = lambda ref: ref.at[pl.ds(XO, NXL), pl.ds(ZO, NZL), :]
    loads = ((eps_h, eps), (psi_h, psi0), (n_h, n_b), (p_h, p_b), (vac_h, i_b), (dop_h, q))
    for k, (source, target) in enumerate(loads):
        for x in range(NXL):
            pltpu.make_async_copy(
                source.at[:, x, :], target.at[XO + x, pl.ds(ZO, NZL), :], load_sem.at[k]
            ).start()

    def loaded(k):
        target = inner(loads[k][1])
        pltpu.make_async_copy(target, target, load_sem.at[k]).wait()

    has = {(0, 0): True}
    has_x = {1: gx < gxs - 1, -1: gx > 0}
    has_z = {1: gz < gzs - 1, -1: gz > 0}

    def exists(direction):
        dx, dz = direction
        if dx == 0:
            return has_z[dz]
        if dz == 0:
            return has_x[dx]
        return jnp.logical_and(has_x[dx], has_z[dz])

    def zero_planes(first):
        for ref in (psi0, eps, q, n_b, p_b, i_b, psi1, psi2):
            for k in range(XO):
                ref[first + k, LO:HI, :] = jnp.zeros((SPAN, NY), F32)

    def zero_rows(first):
        for ref in (psi0, eps, q, n_b, p_b, i_b):
            ref[:, first : first + 8, :] = jnp.zeros((PLANES, 8, NY), F32)

    pl.when(gx == 0)(lambda: zero_planes(0))
    pl.when(gx == gxs - 1)(lambda: zero_planes(XO + NXL))
    pl.when(gz == 0)(lambda: zero_rows(LO))
    pl.when(gz == gzs - 1)(lambda: zero_rows(ZO + NZL))

    def copy_of(name, k):
        buffer, (dx, dz), xs, xd, xc, rs, rd, rc = MESSAGES[name][k]
        ref, at = buffers[buffer], INDEX[name][k]
        return pltpu.make_async_remote_copy(
            src_ref=ref.at[pl.ds(xs, xc), pl.ds(rs, rc), :],
            dst_ref=ref.at[pl.ds(xd, xc), pl.ds(rd, rc), :],
            send_sem=send_sem.at[at],
            recv_sem=recv_sem.at[at],
            device_id=(gx + dx, gz + dz),
            device_id_type=MESH,
        )

    def send(*names):
        for name in names:
            for k, entry in enumerate(MESSAGES[name]):
                pl.when(exists(entry[1]))(lambda name=name, k=k: copy_of(name, k).start())

    def arrived(*names):
        for name in names:
            for k, entry in enumerate(MESSAGES[name]):
                dx, dz = entry[1]
                pl.when(exists((-dx, -dz)))(lambda name=name, k=k: copy_of(name, k).wait_recv())

    def sent(*names):
        for name in names:
            for k, entry in enumerate(MESSAGES[name]):
                pl.when(exists(entry[1]))(lambda name=name, k=k: copy_of(name, k).wait_send())

    loaded(0)
    loaded(1)
    pl.semaphore_wait(barrier, 8)
    send("xpsi", "xeps", "zeps", "zpsi", "dpsi", "deps")

    boundary, _ = layer_counts(layer_ref)
    depth = (lax.broadcasted_iota(jnp.int32, (NZL, NY), 0) + gz * NZL).astype(F32)
    for k in (2, 3, 4, 5):
        loaded(k)

    def charge(x):
        plane = XO + x
        at = (plane, slice(ZO, ZO + NZL))
        level = boundary - height_ref[pl.ds(x, 1), :].astype(F32)
        ions = jnp.where(depth < level, i_b[at], 0.0)
        i_b[at] = ions
        q[at] = 4.0 * (p_b[at] - n_b[at] + ions + q[at])

    blocked(charge, 0, NXL, 2)
    send("zq", "xq", "dq")

    row = lax.broadcasted_iota(jnp.int32, (SPAN, NY), 0)
    above = jnp.where(gz > 0, 0, 8)
    below = jnp.where(gz < gzs - 1, SPAN, SPAN - 8)
    in_z = jnp.logical_and(row >= above, row < below)

    def face_x(plane):
        cx[plane, LO:HI, :] = eps[plane, LO:HI, :] + eps[plane - 1, LO:HI, :]

    def faces(plane):
        mid = eps[plane, LO:HI, :]
        cz[plane, LO:HI, :] = mid + eps[plane, LO - 1 : HI - 1, :]
        cz[plane, HI : HI + 8, :] = eps[plane, HI : HI + 8, :] + eps[plane, HI - 1 : HI + 7, :]
        cy[plane, LO:HI, :] = mid + pltpu.roll(mid, NY - 1, 1)

    def denominator(plane, inside=None):
        side = cy[plane, LO:HI, :]
        total = cx[plane, LO:HI, :] + cx[plane + 1, LO:HI, :] + cz[plane, LO:HI, :]
        total = total + cz[plane, LO + 1 : HI + 1, :] + side + pltpu.roll(side, 1, 1)
        mask = in_z if inside is None else jnp.logical_and(in_z, inside)
        rden[plane, LO:HI, :] = jnp.where(mask, 1.0 / total, 0.0)

    def sweep(source, target):
        def body(plane):
            mid = source[plane, LO:HI, :]
            side = cy[plane, LO:HI, :]
            total = q[plane, LO:HI, :] + cx[plane, LO:HI, :] * source[plane - 1, LO:HI, :]
            total = total + cx[plane + 1, LO:HI, :] * source[plane + 1, LO:HI, :]
            total = total + cz[plane, LO:HI, :] * source[plane, LO - 1 : HI - 1, :]
            total = total + cz[plane, LO + 1 : HI + 1, :] * source[plane, LO + 1 : HI + 1, :]
            total = total + side * pltpu.roll(mid, NY - 1, 1) + pltpu.roll(side * mid, 1, 1)
            target[plane, LO:HI, :] = total * rden[plane, LO:HI, :]

        return body

    arrived("zeps")
    blocked(face_x, XO + 1, NXL - 1, 4)
    blocked(faces, XO, NXL, 4)
    blocked(denominator, XO + 1, NXL - 2, 4)
    arrived("zpsi", "zq")
    both_sides(sweep(psi0, psi1), XO + 1, 2, 12)
    send("xpsi1")
    blocked(sweep(psi0, psi1), XO + 3, 10, 4)
    both_sides(sweep(psi1, psi2), XO + 2, 1, 11)
    send("xpsi2", "xn", "xp", "xi", "zn", "zp", "zi")
    blocked(sweep(psi1, psi2), XO + 3, 10, 4)
    blocked(sweep(psi2, psi3), XO + 3, 10, 4)
    blocked(sweep(psi3, psi4), XO + 4, 8, 4)

    arrived("xeps", "deps")

    def face_x_both(plane):
        face_x(plane)

    both_sides(face_x_both, XO - 2, 3, 18)
    both_sides(faces, XO - 2, 2, 18)

    def denominators(side, carry):
        inside = jnp.where(side == 0, gx > 0, gx < gxs - 1)
        for u in range(3):
            plane = XO - 2 + side * 17 + u
            own = jnp.logical_and(plane >= XO, plane < XO + NXL)
            denominator(plane, jnp.logical_or(own, inside))
        return carry

    lax.fori_loop(0, 2, denominators, 0)
    arrived("xpsi", "dpsi", "xq", "dq")
    both_sides(sweep(psi0, psi1), XO - 1, 2, 16)
    arrived("xpsi1")
    both_sides(sweep(psi1, psi2), XO - 2, 4, 16)
    arrived("xpsi2")
    both_sides(sweep(psi2, psi3), XO - 2, 5, 15)
    both_sides(sweep(psi3, psi4), XO - 1, 5, 13)
    arrived("xn", "xp", "xi", "zn", "zp", "zi")
    sent(*MESSAGES)


def transport_kernel(
    psi, n_b, p_b, i_b, opt_h, layer_ref, height_ref,
    psi_out, n_out, p_out, i_out,
    opt, n_s, p_s, i_s, edge, load_sem, psi_sem, store_sem,
):
    gz = lax.axis_index("gz")
    for x in range(NXL):
        pltpu.make_async_copy(opt_h.at[:, x, :], opt.at[x], load_sem).start()
    for x in range(NXL):
        pltpu.make_async_copy(psi.at[XO + x, pl.ds(ZO, NZL), :], psi_out.at[:, x, :], psi_sem).start()

    boundary, junction = layer_counts(layer_ref)
    depth = (lax.broadcasted_iota(jnp.int32, (NZL, NY), 0) + gz * NZL).astype(F32)

    def flux(a, b):
        u = 0.5 * (b[0] - a[0])
        size = jnp.maximum(jnp.abs(u), TINY)
        mean = size / jnp.tanh(size)
        down, up = mean - u, mean + u
        both = jnp.minimum(a[3], b[3]) > 0.0
        return (
            up * a[1] - down * b[1],
            down * a[2] - up * b[2],
            jnp.where(both, down * a[3] - up * b[3], 0.0),
        )

    fields = (psi, n_b, p_b, i_b)

    def cells(plane, lo, hi):
        return tuple(ref[plane, lo:hi, :] for ref in fields)

    mid = (ZO, ZO + NZL)
    for k, f in enumerate(flux(cells(XO - 1, *mid), cells(XO, *mid))):
        edge[k] = f

    pltpu.make_async_copy(opt, opt, load_sem).wait()

    def plane_of(x):
        plane = XO + x
        here = cells(plane, *mid)
        fx = flux(here, cells(plane + 1, *mid))
        fy = flux(here, tuple(pltpu.roll(f, NY - 1, 1) for f in here))
        fz = flux(cells(plane, ZO - 8, ZO + NZL), cells(plane, ZO - 7, ZO + NZL + 1))
        out = []
        for k in range(3):
            back = pltpu.roll(fz[k], 1, 0)[8:]
            out.append(fx[k] - edge[k] + fy[k] - pltpu.roll(fy[k], 1, 1) + fz[k][8:] - back)
            edge[k] = fx[k]
        _, n, p, i = here
        level = height_ref[pl.ds(x, 1), :].astype(F32)
        rate = jnp.where(depth < boundary - level, 1.0, jnp.where(depth < junction - level, 10.0, 0.2))
        loss = (n * p - 1.0) * rate / (n + p + 2.0)
        gain = 0.05 * (opt[x] - loss)
        n_s[x] = n - 0.04 * out[0] + gain
        p_s[x] = p - 0.03 * out[1] + gain
        i_s[x] = i - 0.02 * out[2]

    def step(x, carry):
        plane_of(x)
        return carry

    lax.fori_loop(0, NXL, step, 0)
    stores = ((n_s, n_out), (p_s, p_out), (i_s, i_out))
    for k, (source, target) in enumerate(stores):
        for x in range(NXL):
            pltpu.make_async_copy(source.at[x], target.at[:, x, :], store_sem.at[k]).start()
    own = psi.at[pl.ds(XO, NXL), pl.ds(ZO, NZL), :]
    pltpu.make_async_copy(own, own, psi_sem).wait()
    for k, (source, target) in enumerate(stores):
        pltpu.make_async_copy(source, source, store_sem.at[k]).wait()


def on_device(psi, n, p, vac, eps, dop, opt, layer, height):
    layer = layer.reshape(8, 128)
    anywhere = pl.BlockSpec(memory_space=pl.ANY)
    near = pl.BlockSpec(memory_space=pltpu.VMEM)
    planes = jax.ShapeDtypeStruct((PLANES, ROWS, NY), F32)
    field = pltpu.VMEM((PLANES, ROWS, NY), F32)
    psi4, n_b, p_b, i_b = pl.pallas_call(
        poisson_kernel,
        out_shape=[planes] * 4,
        in_specs=[anywhere] * 6 + [near] * 2,
        out_specs=[near] * 4,
        scratch_shapes=[field] * 10
        + [
            pltpu.SemaphoreType.DMA((6,)),
            pltpu.SemaphoreType.DMA((COUNT,)),
            pltpu.SemaphoreType.DMA((COUNT,)),
        ],
        compiler_params=pltpu.CompilerParams(
            collective_id=0, has_side_effects=True, vmem_limit_bytes=34 << 20
        ),
        name="poisson",
    )(psi, eps, n, p, vac, dop, layer, height)
    block = jax.ShapeDtypeStruct((NZL, NXL, NY), F32)
    own = pltpu.VMEM((NXL, NZL, NY), F32)
    return pl.pallas_call(
        transport_kernel,
        out_shape=[block] * 4,
        in_specs=[near] * 4 + [anywhere] + [near] * 2,
        out_specs=[anywhere] * 4,
        scratch_shapes=[own] * 4
        + [
            pltpu.VMEM((3, NZL, NY), F32),
            pltpu.SemaphoreType.DMA,
            pltpu.SemaphoreType.DMA,
            pltpu.SemaphoreType.DMA((3,)),
        ],
        compiler_params=pltpu.CompilerParams(vmem_limit_bytes=24 << 20),
        name="transport",
    )(psi4, n_b, p_b, i_b, opt, layer, height)


def solution(mesh):
    grid = P("gz", "gx", None)
    return jax.shard_map(
        on_device,
        mesh=mesh,
        in_specs=(grid,) * 7 + (P(), P("gx", None)),
        out_specs=(grid,) * 4,
        check_vma=False,
    )
```

```python
import functools

import jax
import jax.numpy as jnp
from jax import lax
from jax.experimental import pallas as pl
from jax.experimental.pallas import tpu as pltpu
from jax.sharding import PartitionSpec as P

MESH = pl.DeviceIdType.MESH
F32 = jnp.float32

NXL = 16
NZL = 128
NY = 128
XO = 3
ZO = 16
PLANES = NXL + 2 * XO
ROWS = NZL + 2 * ZO
LO = ZO - 8
HI = ZO + NZL + 8
SPAN = HI - LO
TINY = 1e-10
STEP = 2

XROWS = (ZO, ZO + NZL)
EROWS = (LO, HI)


def x_message(width, first, rows):
    low = XO - first - width
    return (
        ((XO + NXL - first - width, low, width), rows),
        ((XO + first, XO + NXL + first, width), rows),
    )


def row_parts(depth):
    return ((ZO + NZL - depth, ZO - depth, depth), (ZO, ZO + NZL, depth))


def messages():
    table = {}
    for name, buffer, width, first, rows in (
        ("psi", "psi0", 2, 0, XROWS),
        ("eps", "eps", 3, 0, XROWS),
        ("q", "q", 2, 0, XROWS),
        ("n", "n", 1, 0, XROWS),
        ("p", "p", 1, 0, XROWS),
        ("i", "i", 1, 0, XROWS),
        ("psi1", "psi1", 2, 1, EROWS),
        ("psi2", "psi2", 1, 2, EROWS),
    ):
        right, left = x_message(width, first, rows)
        for dx, ((src, dst, count), (lo, hi)) in ((1, right), (-1, left)):
            table.setdefault("x" + name, []).append((buffer, (dx, 0), src, dst, count, lo, lo, hi - lo))
    for name, buffer, depth in (
        ("psi", "psi0", 5),
        ("eps", "eps", 5),
        ("q", "q", 4),
        ("n", "n", 1),
        ("p", "p", 1),
        ("i", "i", 1),
    ):
        for dz, (src, dst, count) in zip((1, -1), row_parts(depth)):
            table.setdefault("z" + name, []).append((buffer, (0, dz), XO, XO, NXL, src, dst, count))
    for name, buffer, width, depth in (("psi", "psi0", 2, 5), ("eps", "eps", 3, 5), ("q", "q", 2, 4)):
        right, left = x_message(width, 0, XROWS)
        for dx, ((xsrc, xdst, xcount), _) in ((1, right), (-1, left)):
            for dz, (src, dst, count) in zip((1, -1), row_parts(depth)):
                table.setdefault("d" + name, []).append((buffer, (dx, dz), xsrc, xdst, xcount, src, dst, count))
    return table


MESSAGES = messages()
INDEX = {}
for _name, _list in MESSAGES.items():
    INDEX[_name] = list(range(sum(map(len, INDEX.values())), sum(map(len, INDEX.values())) + len(_list)))
COUNT = sum(map(len, INDEX.values()))


def blocked(body, first, count, unroll):
    steps = count // unroll
    if steps > 1:

        def step(k, carry):
            for u in range(unroll):
                body(first + k * unroll + u)
            return carry

        lax.fori_loop(0, steps, step, 0)
    else:
        steps = 0
    for u in range(steps * unroll, count):
        body(first + u)


def both_sides(body, first, count, shift):
    def step(side, carry):
        for u in range(count):
            body(first + side * shift + u)
        return carry

    lax.fori_loop(0, 2, step, 0)


def layer_counts(layer_ref):
    kinds = layer_ref[...]

    def total(mask):
        ones = jnp.where(mask, 1.0, 0.0).astype(F32)
        return jnp.sum(jnp.sum(ones, axis=0, keepdims=True), axis=1, keepdims=True)

    return total(kinds == 0), total(kinds <= 1)


def poisson_kernel(
    psi_h, eps_h, n_h, p_h, vac_h, dop_h, opt_h, layer_h, height_h,
    psi4, n_b, p_b, i_b, opt,
    psi0, psi1, psi2, psi3, eps, q, rden, cx, cy, cz, layer_ref, height_ref,
    load_sem, map_sem, send_sem, recv_sem,
):
    gx, gz = lax.axis_index("gx"), lax.axis_index("gz")
    gxs, gzs = lax.axis_size("gx"), lax.axis_size("gz")
    buffers = {"psi0": psi0, "psi1": psi1, "psi2": psi2, "eps": eps, "q": q, "n": n_b, "p": p_b, "i": i_b}

    barrier = pltpu.get_barrier_semaphore()
    for dx in (-1, 0, 1):
        for dz in (-1, 0, 1):
            if dx or dz:
                there = (lax.rem(gx + dx + gxs, gxs), lax.rem(gz + dz + gzs, gzs))
                pl.semaphore_signal(barrier, inc=1, device_id=there, device_id_type=MESH)

    inner = lambda ref: ref.at[pl.ds(XO, NXL), pl.ds(ZO, NZL), :]
    loads = ((eps_h, eps), (psi_h, psi0), (n_h, n_b), (p_h, p_b), (vac_h, i_b), (dop_h, q))
    for k, (source, target) in enumerate(loads):
        for x in range(NXL):
            pltpu.make_async_copy(
                source.at[:, x, :], target.at[XO + x, pl.ds(ZO, NZL), :], load_sem.at[k]
            ).start()

    maps = (
        pltpu.make_async_copy(layer_h, layer_ref, map_sem.at[0]),
        pltpu.make_async_copy(height_h, height_ref, map_sem.at[1]),
    )
    for copy in maps:
        copy.start()
    for x in range(NXL):
        pltpu.make_async_copy(opt_h.at[:, x, :], opt.at[x], load_sem.at[6]).start()

    def loaded(k):
        target = inner(loads[k][1])
        pltpu.make_async_copy(target, target, load_sem.at[k]).wait()

    has = {(0, 0): True}
    has_x = {1: gx < gxs - 1, -1: gx > 0}
    has_z = {1: gz < gzs - 1, -1: gz > 0}

    def exists(direction):
        dx, dz = direction
        if dx == 0:
            return has_z[dz]
        if dz == 0:
            return has_x[dx]
        return jnp.logical_and(has_x[dx], has_z[dz])

    def zero_planes(first):
        for ref in (psi0, eps, q, n_b, p_b, i_b, psi1, psi2):
            for k in range(XO):
                ref[first + k, LO:HI, :] = jnp.zeros((SPAN, NY), F32)

    def zero_rows(first):
        for ref in (psi0, eps, q, n_b, p_b, i_b):
            ref[:, first : first + 8, :] = jnp.zeros((PLANES, 8, NY), F32)

    pl.when(gx == 0)(lambda: zero_planes(0))
    pl.when(gx == gxs - 1)(lambda: zero_planes(XO + NXL))
    pl.when(gz == 0)(lambda: zero_rows(LO))
    pl.when(gz == gzs - 1)(lambda: zero_rows(ZO + NZL))

    def copy_of(name, k):
        buffer, (dx, dz), xs, xd, xc, rs, rd, rc = MESSAGES[name][k]
        ref, at = buffers[buffer], INDEX[name][k]
        return pltpu.make_async_remote_copy(
            src_ref=ref.at[pl.ds(xs, xc), pl.ds(rs, rc), :],
            dst_ref=ref.at[pl.ds(xd, xc), pl.ds(rd, rc), :],
            send_sem=send_sem.at[at],
            recv_sem=recv_sem.at[at],
            device_id=(gx + dx, gz + dz),
            device_id_type=MESH,
        )

    def send(*names):
        for name in names:
            for k, entry in enumerate(MESSAGES[name]):
                pl.when(exists(entry[1]))(lambda name=name, k=k: copy_of(name, k).start())

    def arrived(*names):
        for name in names:
            for k, entry in enumerate(MESSAGES[name]):
                dx, dz = entry[1]
                pl.when(exists((-dx, -dz)))(lambda name=name, k=k: copy_of(name, k).wait_recv())

    def sent(*names):
        for name in names:
            for k, entry in enumerate(MESSAGES[name]):
                pl.when(exists(entry[1]))(lambda name=name, k=k: copy_of(name, k).wait_send())

    loaded(0)
    loaded(1)
    pl.semaphore_wait(barrier, 8)
    send("xpsi", "xeps", "zeps", "zpsi", "dpsi", "deps")

    for copy in maps:
        copy.wait()
    boundary, _ = layer_counts(layer_ref)
    depth = (lax.broadcasted_iota(jnp.int32, (NZL, NY), 0) + gz * NZL).astype(F32)
    for k in (2, 3, 4, 5):
        loaded(k)

    def charge(x):
        plane = XO + x
        at = (plane, slice(ZO, ZO + NZL))
        level = boundary - height_ref[pl.ds(x, 1), :].astype(F32)
        ions = jnp.where(depth < level, i_b[at], 0.0)
        i_b[at] = ions
        q[at] = 4.0 * (p_b[at] - n_b[at] + ions + q[at])

    blocked(charge, 0, NXL, 2)
    send("zq", "xq", "dq")

    row = lax.broadcasted_iota(jnp.int32, (SPAN, NY), 0)
    above = jnp.where(gz > 0, 0, 8)
    below = jnp.where(gz < gzs - 1, SPAN, SPAN - 8)
    in_z = jnp.logical_and(row >= above, row < below)

    def face_x(plane):
        cx[plane, LO:HI, :] = eps[plane, LO:HI, :] + eps[plane - 1, LO:HI, :]

    def faces(plane):
        mid = eps[plane, LO:HI, :]
        cz[plane, LO:HI, :] = mid + eps[plane, LO - 1 : HI - 1, :]
        cz[plane, HI : HI + 8, :] = eps[plane, HI : HI + 8, :] + eps[plane, HI - 1 : HI + 7, :]
        cy[plane, LO:HI, :] = mid + pltpu.roll(mid, NY - 1, 1)

    def denominator(plane, inside=None):
        side = cy[plane, LO:HI, :]
        total = cx[plane, LO:HI, :] + cx[plane + 1, LO:HI, :] + cz[plane, LO:HI, :]
        total = total + cz[plane, LO + 1 : HI + 1, :] + side + pltpu.roll(side, 1, 1)
        mask = in_z if inside is None else jnp.logical_and(in_z, inside)
        rden[plane, LO:HI, :] = jnp.where(mask, 1.0 / total, 0.0)

    def sweep(source, target):
        def body(plane):
            mid = source[plane, LO:HI, :]
            side = cy[plane, LO:HI, :]
            total = q[plane, LO:HI, :] + cx[plane, LO:HI, :] * source[plane - 1, LO:HI, :]
            total = total + cx[plane + 1, LO:HI, :] * source[plane + 1, LO:HI, :]
            total = total + cz[plane, LO:HI, :] * source[plane, LO - 1 : HI - 1, :]
            total = total + cz[plane, LO + 1 : HI + 1, :] * source[plane, LO + 1 : HI + 1, :]
            total = total + side * pltpu.roll(mid, NY - 1, 1) + pltpu.roll(side * mid, 1, 1)
            target[plane, LO:HI, :] = total * rden[plane, LO:HI, :]

        return body

    arrived("zeps")
    blocked(face_x, XO + 1, NXL - 1, 4)
    blocked(faces, XO, NXL, 4)
    blocked(denominator, XO + 1, NXL - 2, 4)
    arrived("zpsi", "zq")
    both_sides(sweep(psi0, psi1), XO + 1, 2, 12)
    send("xpsi1")
    blocked(sweep(psi0, psi1), XO + 3, 10, 4)
    both_sides(sweep(psi1, psi2), XO + 2, 1, 11)
    send("xpsi2", "xn", "xp", "xi", "zn", "zp", "zi")
    blocked(sweep(psi1, psi2), XO + 3, 10, 4)
    blocked(sweep(psi2, psi3), XO + 3, 10, 4)
    blocked(sweep(psi3, psi4), XO + 4, 8, 4)

    arrived("xeps", "deps")

    def face_x_both(plane):
        face_x(plane)

    both_sides(face_x_both, XO - 2, 3, 18)
    both_sides(faces, XO - 2, 2, 18)

    def denominators(side, carry):
        inside = jnp.where(side == 0, gx > 0, gx < gxs - 1)
        for u in range(3):
            plane = XO - 2 + side * 17 + u
            own = jnp.logical_and(plane >= XO, plane < XO + NXL)
            denominator(plane, jnp.logical_or(own, inside))
        return carry

    lax.fori_loop(0, 2, denominators, 0)
    arrived("xpsi", "dpsi", "xq", "dq")
    both_sides(sweep(psi0, psi1), XO - 1, 2, 16)
    arrived("xpsi1")
    both_sides(sweep(psi1, psi2), XO - 2, 4, 16)
    arrived("xpsi2")
    both_sides(sweep(psi2, psi3), XO - 2, 5, 15)
    both_sides(sweep(psi3, psi4), XO - 1, 5, 13)
    arrived("xn", "xp", "xi", "zn", "zp", "zi")
    sent(*MESSAGES)
    pltpu.make_async_copy(opt, opt, load_sem.at[6]).wait()


def transport_kernel(
    psi, n_b, p_b, i_b, opt, layer_h, height_h,
    psi_out, n_out, p_out, i_out,
    n_s, p_s, i_s, edge, layer_ref, height_ref, map_sem, psi_sem, store_sem,
):
    gz = lax.axis_index("gz")
    maps = (
        pltpu.make_async_copy(layer_h, layer_ref, map_sem.at[0]),
        pltpu.make_async_copy(height_h, height_ref, map_sem.at[1]),
    )
    for copy in maps:
        copy.start()
    for x in range(NXL):
        pltpu.make_async_copy(psi.at[XO + x, pl.ds(ZO, NZL), :], psi_out.at[:, x, :], psi_sem).start()

    depth = (lax.broadcasted_iota(jnp.int32, (NZL, NY), 0) + gz * NZL).astype(F32)

    def flux(a, b):
        u = 0.5 * (b[0] - a[0])
        size = jnp.maximum(jnp.abs(u), TINY)
        mean = size / jnp.tanh(size)
        down, up = mean - u, mean + u
        both = jnp.minimum(a[3], b[3]) > 0.0
        return (
            up * a[1] - down * b[1],
            down * a[2] - up * b[2],
            jnp.where(both, down * a[3] - up * b[3], 0.0),
        )

    fields = (psi, n_b, p_b, i_b)

    def cells(plane, lo, hi):
        return tuple(ref[plane, lo:hi, :] for ref in fields)

    mid = (ZO, ZO + NZL)
    for k, f in enumerate(flux(cells(XO - 1, *mid), cells(XO, *mid))):
        edge[k] = f
    for copy in maps:
        copy.wait()
    boundary, junction = layer_counts(layer_ref)
    stores = ((n_s, n_out), (p_s, p_out), (i_s, i_out))

    def plane_of(x, before):
        plane = XO + x
        here = cells(plane, *mid)
        fx = flux(here, cells(plane + 1, *mid))
        fy = flux(here, tuple(pltpu.roll(f, NY - 1, 1) for f in here))
        fz = flux(cells(plane, ZO - 8, ZO + NZL), cells(plane, ZO - 7, ZO + NZL + 1))
        out = []
        for k in range(3):
            back = pltpu.roll(fz[k], 1, 0)[8:]
            out.append(fx[k] - before[k] + fy[k] - pltpu.roll(fy[k], 1, 1) + fz[k][8:] - back)
        _, n, p, i = here
        level = height_ref[pl.ds(x, 1), :].astype(F32)
        rate = jnp.where(depth < boundary - level, 1.0, jnp.where(depth < junction - level, 10.0, 0.2))
        loss = (n * p - 1.0) * rate / (n + p + 2.0)
        gain = 0.05 * (opt[x] - loss)
        n_s[x] = n - 0.04 * out[0] + gain
        p_s[x] = p - 0.03 * out[1] + gain
        i_s[x] = i - 0.02 * out[2]
        return fx

    def step(k, carry):
        fx = tuple(edge[m] for m in range(3))
        for u in range(STEP):
            fx = plane_of(k * STEP + u, fx)
        for m in range(3):
            edge[m] = fx[m]
        for u in range(STEP):
            x = k * STEP + u
            for m, (source, target) in enumerate(stores):
                pltpu.make_async_copy(source.at[x], target.at[:, x, :], store_sem.at[m]).start()
        return carry

    lax.fori_loop(0, NXL // STEP, step, 0)
    own = psi.at[pl.ds(XO, NXL), pl.ds(ZO, NZL), :]
    pltpu.make_async_copy(own, own, psi_sem).wait()
    for k, (source, target) in enumerate(stores):
        pltpu.make_async_copy(source, source, store_sem.at[k]).wait()


def on_device(psi, n, p, vac, eps, dop, opt, layer, height):
    layer = layer.reshape(8, 128)
    far = lambda *arrays: [pltpu.with_memory_space_constraint(a, pltpu.HBM) for a in arrays]
    psi, n, p, vac, eps, dop, opt, layer, height = far(psi, n, p, vac, eps, dop, opt, layer, height)
    anywhere = pl.BlockSpec(memory_space=pltpu.HBM)
    near = pl.BlockSpec(memory_space=pltpu.VMEM)
    maps = [pltpu.VMEM((8, 128), jnp.int32), pltpu.VMEM((NXL, NY), jnp.int32)]
    planes = jax.ShapeDtypeStruct((PLANES, ROWS, NY), F32)
    field = pltpu.VMEM((PLANES, ROWS, NY), F32)
    psi4, n_b, p_b, i_b, light = pl.pallas_call(
        poisson_kernel,
        out_shape=[planes] * 4 + [jax.ShapeDtypeStruct((NXL, NZL, NY), F32)],
        in_specs=[anywhere] * 9,
        out_specs=[near] * 5,
        scratch_shapes=[field] * 10
        + maps
        + [
            pltpu.SemaphoreType.DMA((7,)),
            pltpu.SemaphoreType.DMA((2,)),
            pltpu.SemaphoreType.DMA((COUNT,)),
            pltpu.SemaphoreType.DMA((COUNT,)),
        ],
        compiler_params=pltpu.CompilerParams(
            collective_id=0, has_side_effects=True, vmem_limit_bytes=34 << 20
        ),
        name="poisson",
    )(psi, eps, n, p, vac, dop, opt, layer, height)
    block = jax.ShapeDtypeStruct((NZL, NXL, NY), F32)
    own = pltpu.VMEM((NXL, NZL, NY), F32)
    return pl.pallas_call(
        transport_kernel,
        out_shape=[block] * 4,
        in_specs=[near] * 5 + [anywhere] * 2,
        out_specs=[anywhere] * 4,
        scratch_shapes=[own] * 3
        + [
            pltpu.VMEM((3, NZL, NY), F32),
            *maps,
            pltpu.SemaphoreType.DMA((2,)),
            pltpu.SemaphoreType.DMA,
            pltpu.SemaphoreType.DMA((3,)),
        ],
        compiler_params=pltpu.CompilerParams(vmem_limit_bytes=24 << 20),
        name="transport",
    )(psi4, n_b, p_b, i_b, light, layer, height)


def solution(mesh):
    grid = P("gz", "gx", None)
    return jax.shard_map(
        on_device,
        mesh=mesh,
        in_specs=(grid,) * 7 + (P(), P("gx", None)),
        out_specs=(grid,) * 4,
        check_vma=False,
    )
```

```python
import functools

import jax
import jax.numpy as jnp
from jax import lax
from jax.experimental import pallas as pl
from jax.experimental.pallas import tpu as pltpu
from jax.sharding import PartitionSpec as P

MESH = pl.DeviceIdType.MESH
F32 = jnp.float32

NXL = 16
NZL = 128
NY = 128
XO = 3
ZO = 16
PLANES = NXL + 2 * XO
ROWS = NZL + 2 * ZO
LO = ZO - 8
HI = ZO + NZL + 8
SPAN = HI - LO
TINY = 1e-10
EARLY = 5
DONE = 6

XROWS = (ZO, ZO + NZL)


def x_message(width, first, rows):
    low = XO - first - width
    return (
        ((XO + NXL - first - width, low, width), rows),
        ((XO + first, XO + NXL + first, width), rows),
    )


def row_parts(depth):
    return ((ZO + NZL - depth, ZO - depth, depth), (ZO, ZO + NZL, depth))


def messages():
    table = {}
    for name, buffer, width, first, rows in (
        ("psi", "psi0", 2, 0, XROWS),
        ("eps", "eps", 2, 0, XROWS),
        ("q", "q", 1, 0, XROWS),
        ("n", "n", 1, 0, XROWS),
        ("p", "p", 1, 0, XROWS),
        ("i", "i", 1, 0, XROWS),
        ("psi1", "psi1", 1, 1, (ZO - 3, ZO + NZL + 3)),
        ("rden", "rden", 1, 1, (ZO - 2, ZO + NZL + 2)),
    ):
        right, left = x_message(width, first, rows)
        for dx, ((src, dst, count), (lo, hi)) in ((1, right), (-1, left)):
            table.setdefault("x" + name, []).append((buffer, (dx, 0), src, dst, count, lo, lo, hi - lo))
    for name, level, depth in (("part1", 0, 2), ("part2", 1, 1)):
        for dx, side in ((1, 0), (-1, 1)):
            rows = (ZO - depth, ZO - depth, NZL + 2 * depth)
            table.setdefault("x" + name, []).append(("part", (dx, 0), 2 * side + level, 4 + 2 * side + level, 1) + rows)
    for name, buffer, depth in (
        ("psi", "psi0", 5),
        ("eps", "eps", 5),
        ("q", "q", 4),
        ("n", "n", 1),
        ("p", "p", 1),
        ("i", "i", 1),
    ):
        for dz, (src, dst, count) in zip((1, -1), row_parts(depth)):
            table.setdefault("z" + name, []).append((buffer, (0, dz), XO, XO, NXL, src, dst, count))
    for name, buffer, width, depth in (("psi", "psi0", 2, 5), ("eps", "eps", 2, 5), ("q", "q", 1, 4)):
        right, left = x_message(width, 0, XROWS)
        for dx, ((xsrc, xdst, xcount), _) in ((1, right), (-1, left)):
            for dz, (src, dst, count) in zip((1, -1), row_parts(depth)):
                table.setdefault("d" + name, []).append((buffer, (dx, dz), xsrc, xdst, xcount, src, dst, count))
    return table


MESSAGES = messages()
INDEX = {}
for _name, _list in MESSAGES.items():
    INDEX[_name] = list(range(sum(map(len, INDEX.values())), sum(map(len, INDEX.values())) + len(_list)))
COUNT = sum(map(len, INDEX.values()))


def blocked(body, first, count, unroll):
    steps = count // unroll
    if steps > 1:

        def step(k, carry):
            for u in range(unroll):
                body(first + k * unroll + u)
            return carry

        lax.fori_loop(0, steps, step, 0)
    else:
        steps = 0
    for u in range(steps * unroll, count):
        body(first + u)


def both_sides(body, first, count, shift):
    def step(side, carry):
        for u in range(count):
            body(first + side * shift + u)
        return carry

    lax.fori_loop(0, 2, step, 0)


def layer_counts(layer_ref):
    kinds = layer_ref[...]

    def total(mask):
        ones = jnp.where(mask, 1.0, 0.0).astype(F32)
        return jnp.sum(jnp.sum(ones, axis=0, keepdims=True), axis=1, keepdims=True)

    return total(kinds == 0), total(kinds <= 1)


def poisson_kernel(
    psi_h, eps_h, n_h, p_h, vac_h, dop_h, opt_h, layer_h, height_h,
    psi4, n_b, p_b, i_b, opt, n_s, p_s, i_s,
    psi0, psi1, psi2, psi3, eps, q, rden, cx, cy, cz, part, layer_ref, height_ref,
    load_sem, map_sem, send_sem, recv_sem,
):
    gx, gz = lax.axis_index("gx"), lax.axis_index("gz")
    gxs, gzs = lax.axis_size("gx"), lax.axis_size("gz")
    buffers = {"psi0": psi0, "psi1": psi1, "rden": rden, "part": part, "eps": eps, "q": q, "n": n_b, "p": p_b, "i": i_b}

    has_x = {1: gx < gxs - 1, -1: gx > 0}
    has_z = {1: gz < gzs - 1, -1: gz > 0}

    def exists(direction):
        dx, dz = direction
        if dx == 0:
            return has_z[dz]
        if dz == 0:
            return has_x[dx]
        return jnp.logical_and(has_x[dx], has_z[dz])

    barrier = pltpu.get_barrier_semaphore()
    for dx in (-1, 0, 1):
        for dz in (-1, 0, 1):
            if dx or dz:

                @pl.when(exists((dx, dz)))
                def _(there=(gx + dx, gz + dz)):
                    pl.semaphore_signal(barrier, inc=1, device_id=there, device_id_type=MESH)

    one = lambda flag: jnp.where(flag, 1, 0)
    columns = 1 + one(has_x[1]) + one(has_x[-1])
    beside = columns * (1 + one(has_z[1]) + one(has_z[-1])) - 1

    inner = lambda ref: ref.at[pl.ds(XO, NXL), pl.ds(ZO, NZL), :]
    loads = ((eps_h, eps), (psi_h, psi0), (n_h, n_b), (p_h, p_b), (vac_h, i_b), (dop_h, q))
    for k, (source, target) in enumerate(loads):
        for x in range(NXL):
            pltpu.make_async_copy(
                source.at[:, x, :], target.at[XO + x, pl.ds(ZO, NZL), :], load_sem.at[k]
            ).start()

    maps = (
        pltpu.make_async_copy(layer_h, layer_ref, map_sem.at[0]),
        pltpu.make_async_copy(height_h, height_ref, map_sem.at[1]),
    )
    for copy in maps:
        copy.start()
    for x in range(NXL):
        pltpu.make_async_copy(opt_h.at[:, x, :], opt.at[x], load_sem.at[6]).start()

    def loaded(k):
        target = inner(loads[k][1])
        pltpu.make_async_copy(target, target, load_sem.at[k]).wait()

    def zero_planes(first):
        for ref in (psi0, eps, q, n_b, p_b, i_b, psi1, rden):
            for k in range(XO):
                ref[first + k, LO:HI, :] = jnp.zeros((SPAN, NY), F32)
        for k in range(2):
            part[(4 if first == 0 else 6) + k, LO:HI, :] = jnp.zeros((SPAN, NY), F32)

    def zero_rows(first):
        for ref in (psi0, eps, q, n_b, p_b, i_b):
            ref[:, first : first + 8, :] = jnp.zeros((PLANES, 8, NY), F32)

    pl.when(gx == 0)(lambda: zero_planes(0))
    pl.when(gx == gxs - 1)(lambda: zero_planes(XO + NXL))
    pl.when(gz == 0)(lambda: zero_rows(LO))
    pl.when(gz == gzs - 1)(lambda: zero_rows(ZO + NZL))

    def copy_of(name, k):
        buffer, (dx, dz), xs, xd, xc, rs, rd, rc = MESSAGES[name][k]
        ref, at = buffers[buffer], INDEX[name][k]
        return pltpu.make_async_remote_copy(
            src_ref=ref.at[pl.ds(xs, xc), pl.ds(rs, rc), :],
            dst_ref=ref.at[pl.ds(xd, xc), pl.ds(rd, rc), :],
            send_sem=send_sem.at[at],
            recv_sem=recv_sem.at[at],
            device_id=(gx + dx, gz + dz),
            device_id_type=MESH,
        )

    def send(*names):
        for name in names:
            for k, entry in enumerate(MESSAGES[name]):
                pl.when(exists(entry[1]))(lambda name=name, k=k: copy_of(name, k).start())

    def arrived(*names):
        for name in names:
            for k, entry in enumerate(MESSAGES[name]):
                dx, dz = entry[1]
                pl.when(exists((-dx, -dz)))(lambda name=name, k=k: copy_of(name, k).wait_recv())

    def sent(*names):
        for name in names:
            for k, entry in enumerate(MESSAGES[name]):
                pl.when(exists(entry[1]))(lambda name=name, k=k: copy_of(name, k).wait_send())

    row = lax.broadcasted_iota(jnp.int32, (SPAN, NY), 0) + LO
    above = jnp.where(gz > 0, LO, ZO)
    below = jnp.where(gz < gzs - 1, HI, ZO + NZL)
    in_z = jnp.logical_and(row >= above, row < below)

    def face_x(plane, lo, hi):
        cx[plane, lo:hi, :] = eps[plane, lo:hi, :] + eps[plane - 1, lo:hi, :]

    def faces(plane, lo, hi):
        mid = eps[plane, lo:hi, :]
        cz[plane, lo:hi, :] = mid + eps[plane, lo - 1 : hi - 1, :]
        if hi == HI:
            cz[plane, HI : HI + 8, :] = eps[plane, HI : HI + 8, :] + eps[plane, HI - 1 : HI + 7, :]
        cy[plane, lo:hi, :] = mid + pltpu.roll(mid, NY - 1, 1)

    def denominator(plane, lo, hi, inside=None):
        side = cy[plane, lo:hi, :]
        total = cx[plane, lo:hi, :] + cx[plane + 1, lo:hi, :] + cz[plane, lo:hi, :]
        total = total + cz[plane, lo + 1 : hi + 1, :] + side + pltpu.roll(side, 1, 1)
        mask = in_z[lo - LO : hi - LO]
        if inside is not None:
            mask = jnp.logical_and(mask, inside)
        rden[plane, lo:hi, :] = jnp.where(mask, 1.0 / total, 0.0)

    def sweep(source, target, skip=None, partial=None):
        def body(plane):
            mid = source[plane, LO:HI, :]
            side = cy[plane, LO:HI, :]
            total = q[plane, LO:HI, :] if partial is None else part[partial, LO:HI, :]
            if skip != -1:
                total = total + cx[plane, LO:HI, :] * source[plane - 1, LO:HI, :]
            if skip != 1:
                total = total + cx[plane + 1, LO:HI, :] * source[plane + 1, LO:HI, :]
            total = total + cz[plane, LO:HI, :] * source[plane, LO - 1 : HI - 1, :]
            total = total + cz[plane, LO + 1 : HI + 1, :] * source[plane, LO + 1 : HI + 1, :]
            total = total + side * pltpu.roll(mid, NY - 1, 1) + pltpu.roll(side * mid, 1, 1)
            target[plane, LO:HI, :] = total * rden[plane, LO:HI, :]

        return body

    def partial_sums(level, source):
        for side, plane, face, beyond in ((0, XO + NXL - 2, XO + NXL - 2, XO + NXL - 3), (1, XO + 1, XO + 2, XO + 2)):
            part[2 * side + level, LO:HI, :] = (
                q[plane, LO:HI, :] + cx[face, LO:HI, :] * source[beyond, LO:HI, :]
            )

    loaded(0)
    loaded(1)
    pl.semaphore_wait(barrier, beside)
    send("zeps", "zpsi", "xpsi", "xeps", "dpsi", "deps")

    first, last = ZO + 8, ZO + NZL - 8
    blocked(lambda plane: face_x(plane, *MID), XO + 1, NXL - 1, 4)
    blocked(lambda plane: faces(plane, first, ZO + NZL), XO, NXL, 4)
    blocked(lambda plane: denominator(plane, first, last), XO + 1, NXL - 2, 4)

    loaded(2)
    loaded(3)
    send("xn", "xp")
    for copy in maps:
        copy.wait()
    boundary, junction = layer_counts(layer_ref)
    depth = (lax.broadcasted_iota(jnp.int32, (NZL, NY), 0) + gz * NZL).astype(F32)
    loaded(4)
    loaded(5)

    def charge(x):
        plane = XO + x
        at = (plane, slice(ZO, ZO + NZL))
        level = boundary - height_ref[pl.ds(x, 1), :].astype(F32)
        ions = jnp.where(depth < level, i_b[at], 0.0)
        i_b[at] = ions
        q[at] = 4.0 * (p_b[at] - n_b[at] + ions + q[at])

    blocked(charge, 0, NXL, 2)
    send("zq", "xq", "dq", "zn", "zp", "zi")

    arrived("zeps")

    def rim(body, low, high):
        def both(plane):
            body(plane, LO, low)
            body(plane, high, HI)

        return both

    blocked(rim(face_x, ZO, ZO + NZL), XO + 1, NXL - 1, 4)
    blocked(rim(faces, first, ZO + NZL), XO, NXL, 4)
    blocked(rim(denominator, first, last), XO + 1, NXL - 2, 4)
    send("xrden")
    arrived("zpsi", "zq")
    both_sides(sweep(psi0, psi1), XO + 1, 2, 12)
    partial_sums(0, psi1)
    send("xpsi1", "xpart1")
    both_sides(sweep(psi0, psi1), XO + 3, 1, 9)
    both_sides(sweep(psi1, psi2), XO + 2, 1, 11)
    partial_sums(1, psi2)
    send("xpart2", "xi")
    blocked(sweep(psi0, psi1), XO + 4, 8, 4)
    blocked(sweep(psi1, psi2), XO + 3, 10, 4)
    blocked(sweep(psi2, psi3), XO + 3, 10, 4)
    blocked(sweep(psi3, psi4), XO + 4, 8, 4)

    pltpu.make_async_copy(opt, opt, load_sem.at[6]).wait()
    arrived("zn", "zp", "zi")
    fields = (psi4, n_b, p_b, i_b)
    update = updater(fields, opt, height_ref, boundary, junction, depth)

    def finish(k, flow):
        for u in range(2):
            flow, result = update(EARLY + 2 * k + u, flow)
            for ref, value in zip((n_s, p_s, i_s), result):
                ref[2 * k + u] = value
        return flow

    lax.fori_loop(0, DONE // 2, finish, face_flow(fields, EARLY))

    arrived("xeps", "deps")
    both_sides(lambda plane: face_x(plane, LO, HI), XO - 1, 2, 17)
    both_sides(lambda plane: faces(plane, LO, HI), XO - 2, 2, 18)

    def denominators(side, carry):
        inside = jnp.where(side == 0, gx > 0, gx < gxs - 1)
        for u in range(2):
            plane = XO - 1 + side * 16 + u
            own = jnp.logical_and(plane >= XO, plane < XO + NXL)
            denominator(plane, LO, HI, jnp.logical_or(own, inside))
        return carry

    lax.fori_loop(0, 2, denominators, 0)
    arrived("xpsi", "dpsi", "xq", "dq")
    both_sides(sweep(psi0, psi1), XO - 1, 2, 16)
    arrived("xrden", "xpsi1", "xpart1")
    both_sides(sweep(psi1, psi2), XO - 1, 3, 15)
    sweep(psi1, psi2, -1, 4)(XO - 2)
    sweep(psi1, psi2, 1, 6)(XO + NXL + 1)
    arrived("xpart2")
    both_sides(sweep(psi2, psi3), XO - 1, 4, 14)
    sweep(psi2, psi3, -1, 5)(XO - 2)
    sweep(psi2, psi3, 1, 7)(XO + NXL + 1)
    both_sides(sweep(psi3, psi4), XO - 1, 5, 13)
    arrived("xn", "xp", "xi")
    sent(*MESSAGES)


def flux(a, b):
    u = 0.5 * (b[0] - a[0])
    size = jnp.maximum(jnp.abs(u), TINY)
    mean = size / jnp.tanh(size)
    down, up = mean - u, mean + u
    both = jnp.minimum(a[3], b[3]) > 0.0
    return (
        up * a[1] - down * b[1],
        down * a[2] - up * b[2],
        jnp.where(both, down * a[3] - up * b[3], 0.0),
    )


def cells(fields, plane, lo, hi):
    return tuple(ref[plane, lo:hi, :] for ref in fields)


MID = (ZO, ZO + NZL)


def face_flow(fields, x):
    return flux(cells(fields, XO + x - 1, *MID), cells(fields, XO + x, *MID))


def updater(fields, opt, height_ref, boundary, junction, depth):
    def update(x, before):
        plane = XO + x
        here = cells(fields, plane, *MID)
        fx = flux(here, cells(fields, plane + 1, *MID))
        fy = flux(here, tuple(pltpu.roll(f, NY - 1, 1) for f in here))
        fz = flux(cells(fields, plane, ZO - 8, ZO + NZL), cells(fields, plane, ZO - 7, ZO + NZL + 1))
        out = []
        for k in range(3):
            back = pltpu.roll(fz[k], 1, 0)[8:]
            out.append(fx[k] - before[k] + fy[k] - pltpu.roll(fy[k], 1, 1) + fz[k][8:] - back)
        _, n, p, i = here
        level = height_ref[pl.ds(x, 1), :].astype(F32)
        rate = jnp.where(depth < boundary - level, 1.0, jnp.where(depth < junction - level, 10.0, 0.2))
        loss = (n * p - 1.0) * rate / (n + p + 2.0)
        gain = 0.05 * (opt[x] - loss)
        return fx, (n - 0.04 * out[0] + gain, p - 0.03 * out[1] + gain, i - 0.02 * out[2])

    return update


def transport_kernel(
    psi, n_b, p_b, i_b, opt, n_d, p_d, i_d, layer_h, height_h,
    psi_out, n_out, p_out, i_out,
    n_s, p_s, i_s, layer_ref, height_ref, map_sem, psi_sem, store_sem,
):
    gz = lax.axis_index("gz")
    maps = (
        pltpu.make_async_copy(layer_h, layer_ref, map_sem.at[0]),
        pltpu.make_async_copy(height_h, height_ref, map_sem.at[1]),
    )
    for copy in maps:
        copy.start()
    for x in range(NXL):
        pltpu.make_async_copy(psi.at[XO + x, pl.ds(ZO, NZL), :], psi_out.at[:, x, :], psi_sem).start()
    stores = ((n_s, n_d, n_out), (p_s, p_d, p_out), (i_s, i_d, i_out))
    for m, (_, done, target) in enumerate(stores):
        for k in range(DONE):
            pltpu.make_async_copy(done.at[k], target.at[:, EARLY + k, :], store_sem.at[m]).start()

    depth = (lax.broadcasted_iota(jnp.int32, (NZL, NY), 0) + gz * NZL).astype(F32)
    fields = (psi, n_b, p_b, i_b)
    for copy in maps:
        copy.wait()
    boundary, junction = layer_counts(layer_ref)
    update = updater(fields, opt, height_ref, boundary, junction, depth)

    def step(side, carry):
        first = side * (EARLY + DONE)
        flow = face_flow(fields, first)
        for u in range(EARLY):
            x = first + u
            flow, result = update(x, flow)
            for m, (source, _, target) in enumerate(stores):
                source[x] = result[m]
                pltpu.make_async_copy(source.at[x], target.at[:, x, :], store_sem.at[m]).start()
        return carry

    lax.fori_loop(0, 2, step, 0)
    own = psi.at[pl.ds(XO, NXL), pl.ds(ZO, NZL), :]
    pltpu.make_async_copy(own, own, psi_sem).wait()
    for k, (source, _, target) in enumerate(stores):
        pltpu.make_async_copy(source, source, store_sem.at[k]).wait()


def on_device(psi, n, p, vac, eps, dop, opt, layer, height):
    layer = layer.reshape(8, 128)
    far = lambda *arrays: [pltpu.with_memory_space_constraint(a, pltpu.HBM) for a in arrays]
    psi, n, p, vac, eps, dop, opt, layer, height = far(psi, n, p, vac, eps, dop, opt, layer, height)
    anywhere = pl.BlockSpec(memory_space=pltpu.HBM)
    near = pl.BlockSpec(memory_space=pltpu.VMEM)
    maps = [pltpu.VMEM((8, 128), jnp.int32), pltpu.VMEM((NXL, NY), jnp.int32)]
    planes = jax.ShapeDtypeStruct((PLANES, ROWS, NY), F32)
    field = pltpu.VMEM((PLANES, ROWS, NY), F32)
    psi4, n_b, p_b, i_b, light, *done = pl.pallas_call(
        poisson_kernel,
        out_shape=[planes] * 4
        + [jax.ShapeDtypeStruct((NXL, NZL, NY), F32)]
        + [jax.ShapeDtypeStruct((DONE, NZL, NY), F32)] * 3,
        in_specs=[anywhere] * 9,
        out_specs=[near] * 8,
        scratch_shapes=[field] * 10
        + [pltpu.VMEM((8, ROWS, NY), F32)]
        + maps
        + [
            pltpu.SemaphoreType.DMA((7,)),
            pltpu.SemaphoreType.DMA((2,)),
            pltpu.SemaphoreType.DMA((COUNT,)),
            pltpu.SemaphoreType.DMA((COUNT,)),
        ],
        compiler_params=pltpu.CompilerParams(
            collective_id=0, has_side_effects=True, vmem_limit_bytes=34 << 20
        ),
        name="poisson",
    )(psi, eps, n, p, vac, dop, opt, layer, height)
    block = jax.ShapeDtypeStruct((NZL, NXL, NY), F32)
    own = pltpu.VMEM((NXL, NZL, NY), F32)
    return pl.pallas_call(
        transport_kernel,
        out_shape=[block] * 4,
        in_specs=[near] * 8 + [anywhere] * 2,
        out_specs=[anywhere] * 4,
        scratch_shapes=[own] * 3
        + [
            *maps,
            pltpu.SemaphoreType.DMA((2,)),
            pltpu.SemaphoreType.DMA,
            pltpu.SemaphoreType.DMA((3,)),
        ],
        compiler_params=pltpu.CompilerParams(vmem_limit_bytes=24 << 20),
        name="transport",
    )(psi4, n_b, p_b, i_b, light, *done, layer, height)


def solution(mesh):
    grid = P("gz", "gx", None)
    return jax.shard_map(
        on_device,
        mesh=mesh,
        in_specs=(grid,) * 7 + (P(), P("gx", None)),
        out_specs=(grid,) * 4,
        check_vma=False,
    )
```

```python
import functools

import jax
import jax.numpy as jnp
from jax import lax
from jax.experimental import pallas as pl
from jax.experimental.pallas import tpu as pltpu
from jax.sharding import PartitionSpec as P

MESH = pl.DeviceIdType.MESH
F32 = jnp.float32

NXL = 16
NZL = 128
NY = 128
XO = 3
ZO = 16
PLANES = NXL + 2 * XO
ROWS = NZL + 2 * ZO
LO = ZO - 8
HI = ZO + NZL + 8
SPAN = HI - LO
TINY = 1e-10
DONE = 8

XROWS = (ZO, ZO + NZL)


def x_message(width, first, rows):
    low = XO - first - width
    return (
        ((XO + NXL - first - width, low, width), rows),
        ((XO + first, XO + NXL + first, width), rows),
    )


def row_parts(depth):
    return ((ZO + NZL - depth, ZO - depth, depth), (ZO, ZO + NZL, depth))


def messages():
    table = {}
    for name, buffer, width, first, rows in (
        ("psi", "psi0", 2, 0, XROWS),
        ("eps", "eps", 2, 0, XROWS),
        ("q", "q", 1, 0, XROWS),
        ("n", "n", 1, 0, XROWS),
        ("p", "p", 1, 0, XROWS),
        ("i", "i", 1, 0, XROWS),
        ("psi1", "psi1", 1, 1, (ZO - 3, ZO + NZL + 3)),
        ("rden", "rden", 1, 1, (ZO - 2, ZO + NZL + 2)),
    ):
        right, left = x_message(width, first, rows)
        for dx, ((src, dst, count), (lo, hi)) in ((1, right), (-1, left)):
            table.setdefault("x" + name, []).append((buffer, (dx, 0), src, dst, count, lo, lo, hi - lo))
    for name, level, depth in (("part1", 0, 2), ("part2", 1, 1)):
        for dx, side in ((1, 0), (-1, 1)):
            rows = (ZO - depth, ZO - depth, NZL + 2 * depth)
            table.setdefault("x" + name, []).append(("part", (dx, 0), 2 * side + level, 4 + 2 * side + level, 1) + rows)
    for name, buffer, depth in (
        ("psi", "psi0", 5),
        ("eps", "eps", 5),
        ("q", "q", 4),
        ("n", "n", 1),
        ("p", "p", 1),
        ("i", "i", 1),
    ):
        for dz, (src, dst, count) in zip((1, -1), row_parts(depth)):
            table.setdefault("z" + name, []).append((buffer, (0, dz), XO, XO, NXL, src, dst, count))
    for name, buffer, width, depth in (("psi", "psi0", 2, 5), ("eps", "eps", 2, 5), ("q", "q", 1, 4)):
        right, left = x_message(width, 0, XROWS)
        for dx, ((xsrc, xdst, xcount), _) in ((1, right), (-1, left)):
            for dz, first in ((-1, ZO - depth), (1, ZO + NZL)):
                table.setdefault("c" + name, []).append((buffer, (dx, 0), xsrc, xdst, xcount, first, first, depth, dz))
    return table


MESSAGES = messages()
INDEX = {}
for _name, _list in MESSAGES.items():
    INDEX[_name] = list(range(sum(map(len, INDEX.values())), sum(map(len, INDEX.values())) + len(_list)))
COUNT = sum(map(len, INDEX.values()))


def blocked(body, first, count, unroll):
    steps = count // unroll
    if steps > 1:

        def step(k, carry):
            for u in range(unroll):
                body(first + k * unroll + u)
            return carry

        lax.fori_loop(0, steps, step, 0)
    else:
        steps = 0
    for u in range(steps * unroll, count):
        body(first + u)


def both_sides(body, first, count, shift):
    def step(side, carry):
        for u in range(count):
            body(first + side * shift + u)
        return carry

    lax.fori_loop(0, 2, step, 0)


def layer_counts(layer_ref):
    kinds = layer_ref[...]

    def total(mask):
        ones = jnp.where(mask, 1.0, 0.0).astype(F32)
        return jnp.sum(jnp.sum(ones, axis=0, keepdims=True), axis=1, keepdims=True)

    return total(kinds == 0), total(kinds <= 1)


def poisson_kernel(
    psi_h, eps_h, n_h, p_h, vac_h, dop_h, opt_h, layer_h, height_h,
    psi4, n_b, p_b, i_b, opt, n_s, p_s, i_s,
    psi0, psi1, psi2, psi3, eps, q, rden, cx, cy, cz, part, layer_ref, height_ref,
    load_sem, map_sem, send_sem, recv_sem,
):
    gx, gz = lax.axis_index("gx"), lax.axis_index("gz")
    gxs, gzs = lax.axis_size("gx"), lax.axis_size("gz")
    buffers = {"psi0": psi0, "psi1": psi1, "rden": rden, "part": part, "eps": eps, "q": q, "n": n_b, "p": p_b, "i": i_b}

    has_x = {1: gx < gxs - 1, -1: gx > 0}
    has_z = {1: gz < gzs - 1, -1: gz > 0}

    def exists(dx, dz):
        return has_x[dx] if dx else has_z[dz]

    barrier = pltpu.get_barrier_semaphore()
    for dx, dz in ((-1, 0), (1, 0), (0, -1), (0, 1)):

        @pl.when(exists(dx, dz))
        def _(there=(gx + dx, gz + dz)):
            pl.semaphore_signal(barrier, inc=1, device_id=there, device_id_type=MESH)

    one = lambda flag: jnp.where(flag, 1, 0)
    beside = one(has_x[1]) + one(has_x[-1]) + one(has_z[1]) + one(has_z[-1])

    inner = lambda ref: ref.at[pl.ds(XO, NXL), pl.ds(ZO, NZL), :]
    loads = ((eps_h, eps), (psi_h, psi0), (n_h, n_b), (p_h, p_b), (vac_h, i_b), (dop_h, q))
    for k, (source, target) in enumerate(loads):
        for x in range(NXL):
            pltpu.make_async_copy(
                source.at[:, x, :], target.at[XO + x, pl.ds(ZO, NZL), :], load_sem.at[k]
            ).start()

    maps = (
        pltpu.make_async_copy(layer_h, layer_ref, map_sem.at[0]),
        pltpu.make_async_copy(height_h, height_ref, map_sem.at[1]),
    )
    for copy in maps:
        copy.start()
    for x in range(NXL):
        pltpu.make_async_copy(opt_h.at[:, x, :], opt.at[x], load_sem.at[6]).start()

    def loaded(k):
        target = inner(loads[k][1])
        pltpu.make_async_copy(target, target, load_sem.at[k]).wait()

    def zero_planes(first):
        for ref in (psi0, eps, q, n_b, p_b, i_b, psi1, rden):
            for k in range(XO):
                ref[first + k, LO:HI, :] = jnp.zeros((SPAN, NY), F32)
        for k in range(2):
            part[(4 if first == 0 else 6) + k, LO:HI, :] = jnp.zeros((SPAN, NY), F32)

    def zero_rows(first):
        for ref in (psi0, eps, q, n_b, p_b, i_b):
            ref[:, first : first + 8, :] = jnp.zeros((PLANES, 8, NY), F32)

    pl.when(gx == 0)(lambda: zero_planes(0))
    pl.when(gx == gxs - 1)(lambda: zero_planes(XO + NXL))
    pl.when(gz == 0)(lambda: zero_rows(LO))
    pl.when(gz == gzs - 1)(lambda: zero_rows(ZO + NZL))

    def copy_of(name, k):
        buffer, (dx, dz), xs, xd, xc, rs, rd, rc = MESSAGES[name][k][:8]
        ref, at = buffers[buffer], INDEX[name][k]
        return pltpu.make_async_remote_copy(
            src_ref=ref.at[pl.ds(xs, xc), pl.ds(rs, rc), :],
            dst_ref=ref.at[pl.ds(xd, xc), pl.ds(rd, rc), :],
            send_sem=send_sem.at[at],
            recv_sem=recv_sem.at[at],
            device_id=(gx + dx, gz + dz),
            device_id_type=MESH,
        )

    def when(entry, sender, action, side=None):
        dx, dz = entry[1] if sender else (-entry[1][0], -entry[1][1])
        flag = exists(dx, dz)
        if len(entry) > 8:
            flag = jnp.logical_and(flag, has_z[entry[8]])
        if side is not None:
            flag = jnp.logical_and(flag, side == (0 if dx < 0 else 1))
        pl.when(flag)(action)

    def send(*names):
        for name in names:
            for k, entry in enumerate(MESSAGES[name]):
                when(entry, True, lambda name=name, k=k: copy_of(name, k).start())

    def arrived(*names, side=None):
        for name in names:
            for k, entry in enumerate(MESSAGES[name]):
                when(entry, False, lambda name=name, k=k: copy_of(name, k).wait_recv(), side)

    def sent(*names):
        for name in names:
            for k, entry in enumerate(MESSAGES[name]):
                when(entry, True, lambda name=name, k=k: copy_of(name, k).wait_send())

    row = lax.broadcasted_iota(jnp.int32, (SPAN, NY), 0) + LO
    above = jnp.where(gz > 0, LO, ZO)
    below = jnp.where(gz < gzs - 1, HI, ZO + NZL)
    in_z = jnp.logical_and(row >= above, row < below)

    def face_x(plane, lo, hi):
        cx[plane, lo:hi, :] = eps[plane, lo:hi, :] + eps[plane - 1, lo:hi, :]

    def faces(plane, lo, hi):
        mid = eps[plane, lo:hi, :]
        cz[plane, lo:hi, :] = mid + eps[plane, lo - 1 : hi - 1, :]
        if hi == HI:
            cz[plane, HI : HI + 8, :] = eps[plane, HI : HI + 8, :] + eps[plane, HI - 1 : HI + 7, :]
        cy[plane, lo:hi, :] = mid + pltpu.roll(mid, NY - 1, 1)

    def denominator(plane, lo, hi, inside=None):
        side = cy[plane, lo:hi, :]
        total = cx[plane, lo:hi, :] + cx[plane + 1, lo:hi, :] + cz[plane, lo:hi, :]
        total = total + cz[plane, lo + 1 : hi + 1, :] + side + pltpu.roll(side, 1, 1)
        mask = in_z[lo - LO : hi - LO]
        if inside is not None:
            mask = jnp.logical_and(mask, inside)
        rden[plane, lo:hi, :] = jnp.where(mask, 1.0 / total, 0.0)

    def sweep(source, target, end=None, level=None):
        def body(plane):
            mid = source[plane, LO:HI, :]
            side = cy[plane, LO:HI, :]
            if end is None:
                total = q[plane, LO:HI, :] + cx[plane, LO:HI, :] * source[plane - 1, LO:HI, :]
                total = total + cx[plane + 1, LO:HI, :] * source[plane + 1, LO:HI, :]
            else:
                total = part[4 + 2 * end + level, LO:HI, :]
                total = total + cx[plane + 1 - end, LO:HI, :] * source[plane + 1 - 2 * end, LO:HI, :]
            total = total + cz[plane, LO:HI, :] * source[plane, LO - 1 : HI - 1, :]
            total = total + cz[plane, LO + 1 : HI + 1, :] * source[plane, LO + 1 : HI + 1, :]
            total = total + side * pltpu.roll(mid, NY - 1, 1) + pltpu.roll(side * mid, 1, 1)
            target[plane, LO:HI, :] = total * rden[plane, LO:HI, :]

        return body

    def partial_sums(level, source):
        for side, plane, face, beyond in ((0, XO + NXL - 2, XO + NXL - 2, XO + NXL - 3), (1, XO + 1, XO + 2, XO + 2)):
            part[2 * side + level, LO:HI, :] = (
                q[plane, LO:HI, :] + cx[face, LO:HI, :] * source[beyond, LO:HI, :]
            )

    loaded(0)
    loaded(1)
    pl.semaphore_wait(barrier, beside)
    send("zeps", "zpsi", "xpsi", "xeps")

    first, last = ZO + 8, ZO + NZL - 8
    blocked(lambda plane: face_x(plane, *MID), XO + 1, NXL - 1, 4)
    blocked(lambda plane: faces(plane, first, ZO + NZL), XO, NXL, 4)
    blocked(lambda plane: denominator(plane, first, last), XO + 1, NXL - 2, 4)

    loaded(2)
    loaded(3)
    send("xn", "xp")
    for copy in maps:
        copy.wait()
    boundary, junction = layer_counts(layer_ref)
    depth = (lax.broadcasted_iota(jnp.int32, (NZL, NY), 0) + gz * NZL).astype(F32)
    loaded(4)
    loaded(5)

    def charge(x):
        plane = XO + x
        at = (plane, slice(ZO, ZO + NZL))
        level = boundary - height_ref[pl.ds(x, 1), :].astype(F32)
        ions = jnp.where(depth < level, i_b[at], 0.0)
        i_b[at] = ions
        q[at] = 4.0 * (p_b[at] - n_b[at] + ions + q[at])

    blocked(charge, 0, NXL, 2)
    send("zq", "xq", "zn", "zp", "zi")

    arrived("zeps")
    send("ceps")

    def rim(body, low, high):
        def both(plane):
            body(plane, LO, low)
            body(plane, high, HI)

        return both

    blocked(rim(face_x, ZO, ZO + NZL), XO + 1, NXL - 1, 4)
    blocked(rim(faces, first, ZO + NZL), XO, NXL, 4)
    blocked(rim(denominator, first, last), XO + 1, NXL - 2, 4)
    send("xrden")
    arrived("zpsi", "zq")
    send("cpsi", "cq")
    both_sides(sweep(psi0, psi1), XO + 1, 2, 12)
    partial_sums(0, psi1)
    send("xpsi1", "xpart1")
    both_sides(sweep(psi0, psi1), XO + 3, 1, 9)
    both_sides(sweep(psi1, psi2), XO + 2, 1, 11)
    partial_sums(1, psi2)
    send("xpart2", "xi")
    blocked(sweep(psi0, psi1), XO + 4, 8, 4)
    blocked(sweep(psi1, psi2), XO + 3, 10, 4)
    blocked(sweep(psi2, psi3), XO + 3, 10, 4)
    blocked(sweep(psi3, psi4), XO + 4, 8, 4)

    pltpu.make_async_copy(opt, opt, load_sem.at[6]).wait()
    arrived("zn", "zp", "zi")
    fields = (psi4, n_b, p_b, i_b)
    update = updater(fields, opt, height_ref, boundary, junction, depth)

    def planes(body, first, count):
        for u in range(count):
            body(first + u)

    def beside_face(end):
        arrived("xeps", "ceps", side=end)
        planes(lambda plane: face_x(plane, LO, HI), XO - 1 + 17 * end, 2)
        planes(lambda plane: faces(plane, LO, HI), XO - 2 + 18 * end, 2)
        inside = jnp.where(end == 0, gx, gxs - 1 - gx) > 0
        for u in range(2):
            plane = XO - 1 + 16 * end + u
            own = jnp.logical_and(plane >= XO, plane < XO + NXL)
            denominator(plane, LO, HI, jnp.logical_or(own, inside))
        arrived("xpsi", "cpsi", "xq", "cq", side=end)
        planes(sweep(psi0, psi1), XO - 1 + 16 * end, 2)

    def close_to_face(end):
        outer = XO - 2 + 19 * end
        arrived("xrden", "xpsi1", "xpart1", side=end)
        planes(sweep(psi1, psi2), XO - 1 + 15 * end, 3)
        sweep(psi1, psi2, end, 0)(outer)
        arrived("xpart2", side=end)
        planes(sweep(psi2, psi3), XO - 1 + 14 * end, 4)
        sweep(psi2, psi3, end, 1)(outer)
        planes(sweep(psi3, psi4), XO - 1 + 13 * end, 5)

    near, far = near_end(gx), 1 - near_end(gx)
    beside_face(near)
    close_to_face(near)
    beside_face(far)
    arrived("xn", "xp", "xi", side=near)

    first = (NXL - DONE) * near

    def finish(k, flow):
        for u in range(2):
            flow, result = update(first + 2 * k + u, flow)
            for ref, value in zip((n_s, p_s, i_s), result):
                ref[2 * k + u] = value
        return flow

    flow = lax.fori_loop(0, DONE // 2, finish, face_flow(fields, first))
    if DONE % 2:
        _, result = update(first + DONE - 1, flow)
        for ref, value in zip((n_s, p_s, i_s), result):
            ref[DONE - 1] = value
    close_to_face(far)
    arrived("xn", "xp", "xi", side=far)
    sent(*MESSAGES)


def near_end(gx):
    return 1 - lax.rem(gx, 2)


def flux(a, b):
    u = 0.5 * (b[0] - a[0])
    size = jnp.maximum(jnp.abs(u), TINY)
    mean = size / jnp.tanh(size)
    down, up = mean - u, mean + u
    both = jnp.minimum(a[3], b[3]) > 0.0
    return (
        up * a[1] - down * b[1],
        down * a[2] - up * b[2],
        jnp.where(both, down * a[3] - up * b[3], 0.0),
    )


def cells(fields, plane, lo, hi):
    return tuple(ref[plane, lo:hi, :] for ref in fields)


MID = (ZO, ZO + NZL)


def face_flow(fields, x):
    return flux(cells(fields, XO + x - 1, *MID), cells(fields, XO + x, *MID))


def updater(fields, opt, height_ref, boundary, junction, depth):
    def update(x, before):
        plane = XO + x
        here = cells(fields, plane, *MID)
        fx = flux(here, cells(fields, plane + 1, *MID))
        fy = flux(here, tuple(pltpu.roll(f, NY - 1, 1) for f in here))
        fz = flux(cells(fields, plane, ZO - 8, ZO + NZL), cells(fields, plane, ZO - 7, ZO + NZL + 1))
        out = []
        for k in range(3):
            back = pltpu.roll(fz[k], 1, 0)[8:]
            out.append(fx[k] - before[k] + fy[k] - pltpu.roll(fy[k], 1, 1) + fz[k][8:] - back)
        _, n, p, i = here
        level = height_ref[pl.ds(x, 1), :].astype(F32)
        rate = jnp.where(depth < boundary - level, 1.0, jnp.where(depth < junction - level, 10.0, 0.2))
        loss = (n * p - 1.0) * rate / (n + p + 2.0)
        gain = 0.05 * (opt[x] - loss)
        return fx, (n - 0.04 * out[0] + gain, p - 0.03 * out[1] + gain, i - 0.02 * out[2])

    return update


def transport_kernel(
    psi, n_b, p_b, i_b, opt, n_d, p_d, i_d, layer_h, height_h,
    psi_out, n_out, p_out, i_out,
    n_s, p_s, i_s, layer_ref, height_ref, map_sem, psi_sem, store_sem,
):
    gx, gz = lax.axis_index("gx"), lax.axis_index("gz")
    maps = (
        pltpu.make_async_copy(layer_h, layer_ref, map_sem.at[0]),
        pltpu.make_async_copy(height_h, height_ref, map_sem.at[1]),
    )
    for copy in maps:
        copy.start()
    for x in range(NXL):
        pltpu.make_async_copy(psi.at[XO + x, pl.ds(ZO, NZL), :], psi_out.at[:, x, :], psi_sem).start()
    stores = ((n_s, n_d, n_out), (p_s, p_d, p_out), (i_s, i_d, i_out))
    near = near_end(gx)
    for m, (_, done, target) in enumerate(stores):
        for k in range(DONE):
            x = (NXL - DONE) * near + k
            pltpu.make_async_copy(done.at[k], target.at[:, x, :], store_sem.at[m]).start()

    depth = (lax.broadcasted_iota(jnp.int32, (NZL, NY), 0) + gz * NZL).astype(F32)
    fields = (psi, n_b, p_b, i_b)
    for copy in maps:
        copy.wait()
    boundary, junction = layer_counts(layer_ref)
    update = updater(fields, opt, height_ref, boundary, junction, depth)

    first = DONE * (1 - near)
    flow = face_flow(fields, first)
    for u in range(NXL - DONE):
        x = first + u
        flow, result = update(x, flow)
        for m, (source, _, target) in enumerate(stores):
            source[u] = result[m]
            pltpu.make_async_copy(source.at[u], target.at[:, x, :], store_sem.at[m]).start()
    own = psi.at[pl.ds(XO, NXL), pl.ds(ZO, NZL), :]
    pltpu.make_async_copy(own, own, psi_sem).wait()
    for k, (source, done, _) in enumerate(stores):
        pltpu.make_async_copy(done, done, store_sem.at[k]).wait()
        pltpu.make_async_copy(source, source, store_sem.at[k]).wait()


def on_device(psi, n, p, vac, eps, dop, opt, layer, height):
    layer = layer.reshape(8, 128)
    far = lambda *arrays: [pltpu.with_memory_space_constraint(a, pltpu.HBM) for a in arrays]
    psi, n, p, vac, eps, dop, opt, layer, height = far(psi, n, p, vac, eps, dop, opt, layer, height)
    anywhere = pl.BlockSpec(memory_space=pltpu.HBM)
    near = pl.BlockSpec(memory_space=pltpu.VMEM)
    maps = [pltpu.VMEM((8, 128), jnp.int32), pltpu.VMEM((NXL, NY), jnp.int32)]
    planes = jax.ShapeDtypeStruct((PLANES, ROWS, NY), F32)
    field = pltpu.VMEM((PLANES, ROWS, NY), F32)
    psi4, n_b, p_b, i_b, light, *done = pl.pallas_call(
        poisson_kernel,
        out_shape=[planes] * 4
        + [jax.ShapeDtypeStruct((NXL, NZL, NY), F32)]
        + [jax.ShapeDtypeStruct((DONE, NZL, NY), F32)] * 3,
        in_specs=[anywhere] * 9,
        out_specs=[near] * 8,
        scratch_shapes=[field] * 10
        + [pltpu.VMEM((8, ROWS, NY), F32)]
        + maps
        + [
            pltpu.SemaphoreType.DMA((7,)),
            pltpu.SemaphoreType.DMA((2,)),
            pltpu.SemaphoreType.DMA((COUNT,)),
            pltpu.SemaphoreType.DMA((COUNT,)),
        ],
        compiler_params=pltpu.CompilerParams(
            collective_id=0, has_side_effects=True, vmem_limit_bytes=34 << 20
        ),
        name="poisson",
    )(psi, eps, n, p, vac, dop, opt, layer, height)
    block = jax.ShapeDtypeStruct((NZL, NXL, NY), F32)
    own = pltpu.VMEM((NXL - DONE, NZL, NY), F32)
    return pl.pallas_call(
        transport_kernel,
        out_shape=[block] * 4,
        in_specs=[near] * 8 + [anywhere] * 2,
        out_specs=[anywhere] * 4,
        scratch_shapes=[own] * 3
        + [
            *maps,
            pltpu.SemaphoreType.DMA((2,)),
            pltpu.SemaphoreType.DMA,
            pltpu.SemaphoreType.DMA((3,)),
        ],
        compiler_params=pltpu.CompilerParams(vmem_limit_bytes=24 << 20),
        name="transport",
    )(psi4, n_b, p_b, i_b, light, *done, layer, height)


def solution(mesh):
    grid = P("gz", "gx", None)
    return jax.shard_map(
        on_device,
        mesh=mesh,
        in_specs=(grid,) * 7 + (P(), P("gx", None)),
        out_specs=(grid,) * 4,
        check_vma=False,
    )
```

```python
import functools

import jax
import jax.numpy as jnp
from jax import lax
from jax.experimental import pallas as pl
from jax.experimental.pallas import tpu as pltpu
from jax.sharding import PartitionSpec as P

MESH = pl.DeviceIdType.MESH
F32 = jnp.float32

NXL = 16
NZL = 128
NY = 128
XO = 3
ZO = 16
PLANES = NXL + 2 * XO
ROWS = NZL + 2 * ZO
LO = ZO - 8
HI = ZO + NZL + 8
SPAN = HI - LO
TINY = 1e-10
DONE = 9

XROWS = (ZO, ZO + NZL)


def x_message(width, first, rows):
    low = XO - first - width
    return (
        ((XO + NXL - first - width, low, width), rows),
        ((XO + first, XO + NXL + first, width), rows),
    )


def row_parts(depth):
    return ((ZO + NZL - depth, ZO - depth, depth), (ZO, ZO + NZL, depth))


def messages():
    table = {}
    for name, buffer, width, first, rows in (
        ("psi", "psi0", 2, 0, XROWS),
        ("eps", "eps", 2, 0, XROWS),
        ("q", "q", 1, 0, XROWS),
        ("n", "n", 1, 0, XROWS),
        ("p", "p", 1, 0, XROWS),
        ("i", "i", 1, 0, XROWS),
        ("psi1", "psi1", 1, 1, (ZO - 3, ZO + NZL + 3)),
        ("rden", "rden", 1, 1, (ZO - 2, ZO + NZL + 2)),
    ):
        right, left = x_message(width, first, rows)
        for dx, ((src, dst, count), (lo, hi)) in ((1, right), (-1, left)):
            table.setdefault("x" + name, []).append((buffer, (dx, 0), src, dst, count, lo, lo, hi - lo))
    for name, level, depth in (("part1", 0, 2), ("part2", 1, 1)):
        for dx, side in ((1, 0), (-1, 1)):
            rows = (ZO - depth, ZO - depth, NZL + 2 * depth)
            table.setdefault("x" + name, []).append(("part", (dx, 0), 2 * side + level, 4 + 2 * side + level, 1) + rows)
    for name, buffer, depth in (
        ("psi", "psi0", 5),
        ("eps", "eps", 5),
        ("q", "q", 4),
        ("n", "n", 1),
        ("p", "p", 1),
        ("i", "i", 1),
    ):
        for dz, (src, dst, count) in zip((1, -1), row_parts(depth)):
            table.setdefault("z" + name, []).append((buffer, (0, dz), XO, XO, NXL, src, dst, count))
    for name, buffer, width, depth in (("psi", "psi0", 2, 5), ("eps", "eps", 2, 5), ("q", "q", 1, 4)):
        right, left = x_message(width, 0, XROWS)
        for dx, ((xsrc, xdst, xcount), _) in ((1, right), (-1, left)):
            for dz, first in ((-1, ZO - depth), (1, ZO + NZL)):
                table.setdefault("c" + name, []).append((buffer, (dx, 0), xsrc, xdst, xcount, first, first, depth, dz))
    return table


MESSAGES = messages()
INDEX = {}
for _name, _list in MESSAGES.items():
    INDEX[_name] = list(range(sum(map(len, INDEX.values())), sum(map(len, INDEX.values())) + len(_list)))
COUNT = sum(map(len, INDEX.values()))


def blocked(body, first, count, unroll):
    steps = count // unroll
    if steps > 1:

        def step(k, carry):
            for u in range(unroll):
                body(first + k * unroll + u)
            return carry

        lax.fori_loop(0, steps, step, 0)
    else:
        steps = 0
    for u in range(steps * unroll, count):
        body(first + u)


def both_sides(body, first, count, shift):
    def step(side, carry):
        for u in range(count):
            body(first + side * shift + u)
        return carry

    lax.fori_loop(0, 2, step, 0)


def layer_counts(layer_ref):
    kinds = layer_ref[...]

    def total(mask):
        ones = jnp.where(mask, 1.0, 0.0).astype(F32)
        return jnp.sum(jnp.sum(ones, axis=0, keepdims=True), axis=1, keepdims=True)

    return total(kinds == 0), total(kinds <= 1)


def poisson_kernel(
    psi_h, eps_h, n_h, p_h, vac_h, dop_h, opt_h, layer_h, height_h,
    psi4, n_b, p_b, i_b, opt, layer_ref, height_ref, n_s, p_s, i_s,
    psi0, psi1, psi2, psi3, eps, q, rden, cx, cy, cz, part,
    load_sem, map_sem, send_sem, recv_sem,
):
    gx, gz = lax.axis_index("gx"), lax.axis_index("gz")
    gxs, gzs = lax.axis_size("gx"), lax.axis_size("gz")
    buffers = {"psi0": psi0, "psi1": psi1, "rden": rden, "part": part, "eps": eps, "q": q, "n": n_b, "p": p_b, "i": i_b}

    has_x = {1: gx < gxs - 1, -1: gx > 0}
    has_z = {1: gz < gzs - 1, -1: gz > 0}

    def exists(dx, dz):
        return has_x[dx] if dx else has_z[dz]

    barrier = pltpu.get_barrier_semaphore()
    for dx, dz in ((-1, 0), (1, 0), (0, -1), (0, 1)):

        @pl.when(exists(dx, dz))
        def _(there=(gx + dx, gz + dz)):
            pl.semaphore_signal(barrier, inc=1, device_id=there, device_id_type=MESH)

    one = lambda flag: jnp.where(flag, 1, 0)
    beside = one(has_x[1]) + one(has_x[-1]) + one(has_z[1]) + one(has_z[-1])

    inner = lambda ref: ref.at[pl.ds(XO, NXL), pl.ds(ZO, NZL), :]
    loads = ((eps_h, eps), (psi_h, psi0), (n_h, n_b), (p_h, p_b), (vac_h, i_b), (dop_h, q))
    for k, (source, target) in enumerate(loads):
        for x in range(NXL):
            pltpu.make_async_copy(
                source.at[:, x, :], target.at[XO + x, pl.ds(ZO, NZL), :], load_sem.at[k]
            ).start()

    maps = (
        pltpu.make_async_copy(layer_h, layer_ref, map_sem.at[0]),
        pltpu.make_async_copy(height_h, height_ref, map_sem.at[1]),
    )
    for copy in maps:
        copy.start()

    def loaded(k):
        target = inner(loads[k][1])
        pltpu.make_async_copy(target, target, load_sem.at[k]).wait()

    def zero_planes(first):
        for ref in (psi0, eps, q, n_b, p_b, i_b, psi1, rden):
            for k in range(XO):
                ref[first + k, LO:HI, :] = jnp.zeros((SPAN, NY), F32)
        for k in range(2):
            part[(4 if first == 0 else 6) + k, LO:HI, :] = jnp.zeros((SPAN, NY), F32)

    def zero_rows(first):
        for ref in (psi0, eps, q, n_b, p_b, i_b):
            ref[:, first : first + 8, :] = jnp.zeros((PLANES, 8, NY), F32)

    pl.when(gx == 0)(lambda: zero_planes(0))
    pl.when(gx == gxs - 1)(lambda: zero_planes(XO + NXL))
    pl.when(gz == 0)(lambda: zero_rows(LO))
    pl.when(gz == gzs - 1)(lambda: zero_rows(ZO + NZL))

    def copy_of(name, k):
        buffer, (dx, dz), xs, xd, xc, rs, rd, rc = MESSAGES[name][k][:8]
        ref, at = buffers[buffer], INDEX[name][k]
        return pltpu.make_async_remote_copy(
            src_ref=ref.at[pl.ds(xs, xc), pl.ds(rs, rc), :],
            dst_ref=ref.at[pl.ds(xd, xc), pl.ds(rd, rc), :],
            send_sem=send_sem.at[at],
            recv_sem=recv_sem.at[at],
            device_id=(gx + dx, gz + dz),
            device_id_type=MESH,
        )

    def when(entry, sender, action, side=None):
        dx, dz = entry[1] if sender else (-entry[1][0], -entry[1][1])
        flag = exists(dx, dz)
        if len(entry) > 8:
            flag = jnp.logical_and(flag, has_z[entry[8]])
        if side is not None:
            flag = jnp.logical_and(flag, side == (0 if dx < 0 else 1))
        pl.when(flag)(action)

    def send(*names):
        for name in names:
            for k, entry in enumerate(MESSAGES[name]):
                when(entry, True, lambda name=name, k=k: copy_of(name, k).start())

    def arrived(*names, side=None):
        for name in names:
            for k, entry in enumerate(MESSAGES[name]):
                when(entry, False, lambda name=name, k=k: copy_of(name, k).wait_recv(), side)

    def sent(*names):
        for name in names:
            for k, entry in enumerate(MESSAGES[name]):
                when(entry, True, lambda name=name, k=k: copy_of(name, k).wait_send())

    row = lax.broadcasted_iota(jnp.int32, (SPAN, NY), 0) + LO
    above = jnp.where(gz > 0, LO, ZO)
    below = jnp.where(gz < gzs - 1, HI, ZO + NZL)
    in_z = jnp.logical_and(row >= above, row < below)

    def face_x(plane, lo, hi):
        cx[plane, lo:hi, :] = eps[plane, lo:hi, :] + eps[plane - 1, lo:hi, :]

    def faces(plane, lo, hi):
        mid = eps[plane, lo:hi, :]
        cz[plane, lo:hi, :] = mid + eps[plane, lo - 1 : hi - 1, :]
        if hi == HI:
            cz[plane, HI : HI + 8, :] = eps[plane, HI : HI + 8, :] + eps[plane, HI - 1 : HI + 7, :]
        cy[plane, lo:hi, :] = mid + pltpu.roll(mid, NY - 1, 1)

    def denominator(plane, lo, hi, inside=None):
        side = cy[plane, lo:hi, :]
        total = cx[plane, lo:hi, :] + cx[plane + 1, lo:hi, :] + cz[plane, lo:hi, :]
        total = total + cz[plane, lo + 1 : hi + 1, :] + side + pltpu.roll(side, 1, 1)
        mask = in_z[lo - LO : hi - LO]
        if inside is not None:
            mask = jnp.logical_and(mask, inside)
        rden[plane, lo:hi, :] = jnp.where(mask, 1.0 / total, 0.0)

    def sweep(source, target, end=None, level=None):
        def body(plane):
            mid = source[plane, LO:HI, :]
            side = cy[plane, LO:HI, :]
            if end is None:
                total = q[plane, LO:HI, :] + cx[plane, LO:HI, :] * source[plane - 1, LO:HI, :]
                total = total + cx[plane + 1, LO:HI, :] * source[plane + 1, LO:HI, :]
            else:
                total = part[4 + 2 * end + level, LO:HI, :]
                total = total + cx[plane + 1 - end, LO:HI, :] * source[plane + 1 - 2 * end, LO:HI, :]
            total = total + cz[plane, LO:HI, :] * source[plane, LO - 1 : HI - 1, :]
            total = total + cz[plane, LO + 1 : HI + 1, :] * source[plane, LO + 1 : HI + 1, :]
            total = total + side * pltpu.roll(mid, NY - 1, 1) + pltpu.roll(side * mid, 1, 1)
            target[plane, LO:HI, :] = total * rden[plane, LO:HI, :]

        return body

    def partial_sums(level, source):
        for side, plane, face, beyond in ((0, XO + NXL - 2, XO + NXL - 2, XO + NXL - 3), (1, XO + 1, XO + 2, XO + 2)):
            part[2 * side + level, LO:HI, :] = (
                q[plane, LO:HI, :] + cx[face, LO:HI, :] * source[beyond, LO:HI, :]
            )

    loaded(0)
    loaded(1)
    pl.semaphore_wait(barrier, beside)
    send("zeps", "zpsi", "xpsi", "xeps")

    first, last = ZO + 8, ZO + NZL - 8
    blocked(lambda plane: face_x(plane, *MID), XO + 1, NXL - 1, 4)
    blocked(lambda plane: faces(plane, first, ZO + NZL), XO, NXL, 4)
    blocked(lambda plane: denominator(plane, first, last), XO + 1, NXL - 2, 4)

    loaded(2)
    loaded(3)
    send("xn", "xp")
    for copy in maps:
        copy.wait()
    boundary, junction = layer_counts(layer_ref)
    depth = (lax.broadcasted_iota(jnp.int32, (NZL, NY), 0) + gz * NZL).astype(F32)
    loaded(4)
    loaded(5)

    def charge(x):
        plane = XO + x
        at = (plane, slice(ZO, ZO + NZL))
        level = boundary - height_ref[pl.ds(x, 1), :].astype(F32)
        ions = jnp.where(depth < level, i_b[at], 0.0)
        i_b[at] = ions
        q[at] = 4.0 * (p_b[at] - n_b[at] + ions + q[at])

    blocked(charge, 0, NXL, 2)
    send("zq", "xq", "zn", "zp", "zi")

    for x in range(NXL):
        pltpu.make_async_copy(opt_h.at[:, x, :], opt.at[x], load_sem.at[6]).start()
    arrived("zeps")
    send("ceps")

    def rim(body, low, high):
        def both(plane):
            body(plane, LO, low)
            body(plane, high, HI)

        return both

    blocked(rim(face_x, ZO, ZO + NZL), XO + 1, NXL - 1, 4)
    blocked(rim(faces, first, ZO + NZL), XO, NXL, 4)
    blocked(rim(denominator, first, last), XO + 1, NXL - 2, 4)
    send("xrden")
    arrived("zpsi", "zq")
    send("cpsi", "cq")
    both_sides(sweep(psi0, psi1), XO + 1, 2, 12)
    partial_sums(0, psi1)
    send("xpsi1", "xpart1")
    both_sides(sweep(psi0, psi1), XO + 3, 1, 9)
    both_sides(sweep(psi1, psi2), XO + 2, 1, 11)
    partial_sums(1, psi2)
    send("xpart2", "xi")
    blocked(sweep(psi0, psi1), XO + 4, 8, 4)
    blocked(sweep(psi1, psi2), XO + 3, 10, 4)
    blocked(sweep(psi2, psi3), XO + 3, 10, 4)
    blocked(sweep(psi3, psi4), XO + 4, 8, 4)

    pltpu.make_async_copy(opt, opt, load_sem.at[6]).wait()
    arrived("zn", "zp", "zi")
    fields = (psi4, n_b, p_b, i_b)
    update = updater(fields, opt, height_ref, boundary, junction, depth)

    def planes(body, first, count):
        for u in range(count):
            body(first + u)

    def beside_face(end):
        arrived("xeps", "ceps", side=end)
        planes(lambda plane: face_x(plane, LO, HI), XO - 1 + 17 * end, 2)
        planes(lambda plane: faces(plane, LO, HI), XO - 2 + 18 * end, 2)
        inside = jnp.where(end == 0, gx, gxs - 1 - gx) > 0
        for u in range(2):
            plane = XO - 1 + 16 * end + u
            own = jnp.logical_and(plane >= XO, plane < XO + NXL)
            denominator(plane, LO, HI, jnp.logical_or(own, inside))
        arrived("xpsi", "cpsi", "xq", "cq", side=end)
        planes(sweep(psi0, psi1), XO - 1 + 16 * end, 2)

    def close_to_face(end):
        outer = XO - 2 + 19 * end
        arrived("xrden", "xpsi1", "xpart1", side=end)
        planes(sweep(psi1, psi2), XO - 1 + 15 * end, 3)
        sweep(psi1, psi2, end, 0)(outer)
        arrived("xpart2", side=end)
        planes(sweep(psi2, psi3), XO - 1 + 14 * end, 4)
        sweep(psi2, psi3, end, 1)(outer)
        planes(sweep(psi3, psi4), XO - 1 + 13 * end, 5)

    near, far = near_end(gx), 1 - near_end(gx)
    beside_face(near)
    close_to_face(near)
    beside_face(far)
    arrived("xn", "xp", "xi", side=near)

    first = (NXL - DONE) * near

    def finish(k, flow):
        for u in range(2):
            flow = update(first + 2 * k + u, flow, (n_s, p_s, i_s), 2 * k + u)
        return flow

    flow = lax.fori_loop(0, DONE // 2, finish, face_flow(fields, first))
    if DONE % 2:
        update(first + DONE - 1, flow, (n_s, p_s, i_s), DONE - 1)
    close_to_face(far)
    arrived("xn", "xp", "xi", side=far)
    sent(*MESSAGES)


def near_end(gx):
    return 1 - lax.rem(gx, 2)


def flux(a, b):
    u = 0.5 * (b[0] - a[0])
    size = jnp.maximum(jnp.abs(u), TINY)
    mean = size / jnp.tanh(size)
    down, up = mean - u, mean + u
    both = jnp.minimum(a[3], b[3]) > 0.0
    return (
        up * a[1] - down * b[1],
        down * a[2] - up * b[2],
        jnp.where(both, down * a[3] - up * b[3], 0.0),
    )


def cells(fields, plane, lo, hi):
    return tuple(ref[plane, lo:hi, :] for ref in fields)


MID = (ZO, ZO + NZL)


CHUNK = 64
CHUNKS = tuple((ZO + r, ZO + r + CHUNK) for r in range(0, NZL, CHUNK))


def face_flow(fields, x):
    return tuple(flux(cells(fields, XO + x - 1, *c), cells(fields, XO + x, *c)) for c in CHUNKS)


def updater(fields, opt, height_ref, boundary, junction, depth):
    def update(x, before, targets, at):
        plane = XO + x
        level = height_ref[pl.ds(x, 1), :].astype(F32)
        flow = []
        for (lo, hi), came in zip(CHUNKS, before):
            rows = slice(lo - ZO, hi - ZO)
            here = cells(fields, plane, lo, hi)
            fx = flux(here, cells(fields, plane + 1, lo, hi))
            fy = flux(here, tuple(pltpu.roll(f, NY - 1, 1) for f in here))
            fz = flux(cells(fields, plane, lo - 8, hi), cells(fields, plane, lo - 7, hi + 1))
            out = []
            for k in range(3):
                back = pltpu.roll(fz[k], 1, 0)[8:]
                out.append(fx[k] - came[k] + fy[k] - pltpu.roll(fy[k], 1, 1) + fz[k][8:] - back)
            _, n, p, i = here
            z = depth[rows]
            rate = jnp.where(z < boundary - level, 1.0, jnp.where(z < junction - level, 10.0, 0.2))
            loss = (n * p - 1.0) * rate / (n + p + 2.0)
            gain = 0.05 * (opt[x, rows, :] - loss)
            targets[0][at, rows, :] = n - 0.04 * out[0] + gain
            targets[1][at, rows, :] = p - 0.03 * out[1] + gain
            targets[2][at, rows, :] = i - 0.02 * out[2]
            flow.append(fx)
        return tuple(flow)

    return update


def transport_kernel(
    psi, n_b, p_b, i_b, opt, layer_ref, height_ref, n_d, p_d, i_d,
    psi_out, n_out, p_out, i_out,
    n_s, p_s, i_s, psi_sem, store_sem,
):
    gx, gz = lax.axis_index("gx"), lax.axis_index("gz")
    for x in range(NXL):
        pltpu.make_async_copy(psi.at[XO + x, pl.ds(ZO, NZL), :], psi_out.at[:, x, :], psi_sem).start()
    stores = ((n_s, n_d, n_out), (p_s, p_d, p_out), (i_s, i_d, i_out))
    near = near_end(gx)
    for m, (_, done, target) in enumerate(stores):
        for k in range(DONE):
            x = (NXL - DONE) * near + k
            pltpu.make_async_copy(done.at[k], target.at[:, x, :], store_sem.at[m]).start()

    depth = (lax.broadcasted_iota(jnp.int32, (NZL, NY), 0) + gz * NZL).astype(F32)
    fields = (psi, n_b, p_b, i_b)
    boundary, junction = layer_counts(layer_ref)
    update = updater(fields, opt, height_ref, boundary, junction, depth)

    first = DONE * (1 - near)
    flow = face_flow(fields, first)
    for u in range(NXL - DONE):
        x = first + u
        flow = update(x, flow, (n_s, p_s, i_s), u)
        for m, (source, _, target) in enumerate(stores):
            pltpu.make_async_copy(source.at[u], target.at[:, x, :], store_sem.at[m]).start()
    own = psi.at[pl.ds(XO, NXL), pl.ds(ZO, NZL), :]
    pltpu.make_async_copy(own, own, psi_sem).wait()
    for k, (source, done, _) in enumerate(stores):
        pltpu.make_async_copy(done, done, store_sem.at[k]).wait()
        pltpu.make_async_copy(source, source, store_sem.at[k]).wait()


def on_device(psi, n, p, vac, eps, dop, opt, layer, height):
    layer = layer.reshape(8, 128)
    far = lambda *arrays: [pltpu.with_memory_space_constraint(a, pltpu.HBM) for a in arrays]
    psi, n, p, vac, eps, dop, opt, layer, height = far(psi, n, p, vac, eps, dop, opt, layer, height)
    anywhere = pl.BlockSpec(memory_space=pltpu.HBM)
    near = pl.BlockSpec(memory_space=pltpu.VMEM)
    planes = jax.ShapeDtypeStruct((PLANES, ROWS, NY), F32)
    field = pltpu.VMEM((PLANES, ROWS, NY), F32)
    psi4, n_b, p_b, i_b, light, *rest = pl.pallas_call(
        poisson_kernel,
        out_shape=[planes] * 4
        + [jax.ShapeDtypeStruct((NXL, NZL, NY), F32)]
        + [jax.ShapeDtypeStruct((8, 128), jnp.int32), jax.ShapeDtypeStruct((NXL, NY), jnp.int32)]
        + [jax.ShapeDtypeStruct((DONE, NZL, NY), F32)] * 3,
        in_specs=[anywhere] * 9,
        out_specs=[near] * 10,
        scratch_shapes=[field] * 10
        + [pltpu.VMEM((8, ROWS, NY), F32)]
        + [
            pltpu.SemaphoreType.DMA((7,)),
            pltpu.SemaphoreType.DMA((2,)),
            pltpu.SemaphoreType.DMA((COUNT,)),
            pltpu.SemaphoreType.DMA((COUNT,)),
        ],
        compiler_params=pltpu.CompilerParams(
            collective_id=0, has_side_effects=True, vmem_limit_bytes=34 << 20
        ),
        name="poisson",
    )(psi, eps, n, p, vac, dop, opt, layer, height)
    block = jax.ShapeDtypeStruct((NZL, NXL, NY), F32)
    own = pltpu.VMEM((NXL - DONE, NZL, NY), F32)
    return pl.pallas_call(
        transport_kernel,
        out_shape=[block] * 4,
        in_specs=[near] * 10,
        out_specs=[anywhere] * 4,
        scratch_shapes=[own] * 3
        + [
            pltpu.SemaphoreType.DMA,
            pltpu.SemaphoreType.DMA((3,)),
        ],
        compiler_params=pltpu.CompilerParams(vmem_limit_bytes=24 << 20),
        name="transport",
    )(psi4, n_b, p_b, i_b, light, *rest)


def solution(mesh):
    grid = P("gz", "gx", None)
    return jax.shard_map(
        on_device,
        mesh=mesh,
        in_specs=(grid,) * 7 + (P(), P("gx", None)),
        out_specs=(grid,) * 4,
        check_vma=False,
    )
```
